256 devices in a mesh: light: 16 (over y, x), depth: 2 (over core), height: 8 (over z).
Axes of the slice: x: 4, y: 4, z: 8, core: 2. Of those that a mesh axis runs over, the one named last changes fastest.
Arguments:
- density: float32 [256, 32, 4096], P('light', 'depth', 'height'), may hold values from 0 to 6.4
- active_list: int32 [4, 384], P('depth'), may hold values from -1 to 511, as said below
- light_dir: int32 [8], replicated, may hold values from 0 to 1, as said below
- lamp_plane: float32 [8, 32, 4096], P(None, 'depth', 'height'), may hold values from 0.5 to 2
- extinction: float32 [8], replicated, may hold values from 0.00390625 to 0.01953125
- blur_weights: float32 [8, 25], replicated, may hold values from 0.2 to 16
- albedo: float32 [8], replicated, may hold values from 0.3 to 1
Outputs:
- rendered: float32 [8, 256, 4096], P('depth', 'light', 'height')
The draws below stay inside these ranges and needn't reach their ends.
Inputs may be any that keep to these rules, and one draw needn't show every extreme that they name: `active_list`: each row lists distinct brick numbers lb * 32 + hb (lb the light slab of 16 slices, hb the height brick of 128 cells) of one depth slab of 8 cells, then -1 to its end; a row lists between 192 and 384 bricks, and some row lists 384. `light_dir`: exactly 4 entries are 1.
All inputs are finite; a program needn't handle non-finite values.
Results may differ from the reference program's by a relative error of at most 0.00016.
Values sent between devices are 32-bit elements; how exact they have to be, the bound alone decides.
A program may use at most 64 MiB of HBM per device.

```python
import math
import jax
import jax.numpy as jnp
from jax import lax

C = 8
LS = 16
BZ = 8
BH = 128
NL = 256
NZ = 32
NH = 4096
NHB = 32
NZB = 4
BRICKS = 512
SLOTS = 384


def draw_active_list(key, part):
    slab_keys = jax.random.split(jax.random.fold_in(key, 11), NZB)

    def one_slab(slab_key):
        shuffled = jax.random.permutation(slab_key, BRICKS).astype(jnp.int32)
        listed_count = jax.random.randint(jax.random.fold_in(slab_key, 3), (), SLOTS // 2, SLOTS + 1)
        return (shuffled[:SLOTS], listed_count)
    shuffled_rows, counts = jax.vmap(one_slab)(slab_keys)
    counts = counts.at[0].set(SLOTS)
    slot_index = jnp.arange(SLOTS, dtype=jnp.int32)
    return jnp.where(slot_index[None, :] < counts[:, None], shuffled_rows, -1).astype(jnp.int32)


def draw_light_dir(key, part):
    shuffled = jax.random.permutation(jax.random.fold_in(key, 7), C)
    return (shuffled >= C // 2).astype(jnp.int32)


def draw_density(key, part):
    slab_count = NL // LS
    low = jnp.log(jnp.float32(0.25))
    high = jnp.log(jnp.float32(2.0))
    along_height = jnp.exp(jax.random.uniform(jax.random.fold_in(key, 31), (slab_count, 1, NH), jnp.float32, low, high))
    along_depth = jnp.exp(jax.random.uniform(jax.random.fold_in(key, 32), (slab_count, NZ, 1), jnp.float32, low, high))
    cells = jax.random.uniform(jax.random.fold_in(key, 33), (slab_count, LS, NZ, NH), jnp.float32, 0.5, 1.5)
    factor = along_height * along_depth
    return (cells * factor[:, None]).reshape(NL, NZ, NH).astype(jnp.float32)


def draw_blur_weights(key, part):
    beside_all = jax.random.uniform(jax.random.fold_in(key, 41), (C, 25), jnp.float32, 0.2, 1.0)
    centre = jax.random.uniform(jax.random.fold_in(key, 42), (C,), jnp.float32, 8.0, 16.0)
    return beside_all.at[:, 12].set(centre).astype(jnp.float32)


def block_levels(key, dims, pieces, low, high):
    level, own = 1.0, jax.random.fold_in(key, 6)
    for dim, parts in pieces:
        steps = jnp.exp(jax.random.uniform(jax.random.fold_in(own, dim), (parts,), jnp.float32, low / len(pieces), high / len(pieces)))
        level = level * jnp.repeat(steps, dims[dim] // parts).reshape([-1 if axis == dim else 1 for axis in range(len(dims))])
    return level


def setup_inputs(seed: int = 0) -> dict:
    arg_keys = jax.random.split(jax.random.key(seed), 8)
    return {
        "density": draw_density(jax.random.fold_in(arg_keys[7], 71), 0),
        "active_list": draw_active_list(jax.random.fold_in(arg_keys[7], 71), 0),
        "light_dir": draw_light_dir(jax.random.fold_in(arg_keys[7], 71), 0),
        "lamp_plane": jnp.clip(0.5 + 1.5 * jax.random.uniform(arg_keys[3], (C, NZ, NH), jnp.float32) ** block_levels(arg_keys[3], (C, NZ, NH), ((1, 2), (2, 8)), -0.2, 0.2), 0.5, 2.0),
        "extinction": jnp.clip(jnp.exp(jax.random.uniform(arg_keys[4], (C,), jnp.float32, math.log(0.00390625), math.log(0.01953125))), 0.00390625, 0.01953125),
        "blur_weights": draw_blur_weights(jax.random.fold_in(arg_keys[7], 71), 0),
        "albedo": jnp.clip(jax.random.uniform(arg_keys[6], (C,), jnp.float32, 0.3, 1.0), 0.3, 1.0),
    }


def blur_plane(plane_in, kernel):
    depth_len = plane_in.shape[1]
    height_len = plane_in.shape[2]
    padded = jnp.pad(plane_in, ((0, 0), (2, 2), (2, 2)))
    total = jnp.zeros_like(plane_in)
    for row_off in range(5):
        for col_off in range(5):
            total = total + kernel[:, row_off, col_off, None, None] * padded[:, row_off:row_off + depth_len, col_off:col_off + height_len]
    return total


def live_cells(active_list):
    brick_ids = jnp.arange(BRICKS, dtype=jnp.int32)
    listed = jnp.any(active_list[:, :, None] == brick_ids[None, None, :], axis=1).astype(jnp.float32)
    listed = listed.reshape(NZB, NL // LS, NHB).transpose(1, 0, 2)
    return jnp.repeat(jnp.repeat(jnp.repeat(listed, LS, 0), BZ, 1), BH, 2)


def march(masked, lamp_plane, extinction, kernel, albedo):
    slabs = masked.reshape(NL // LS, LS, NZ, NH)

    def slab_step(plane_in, slab):
        before = jnp.cumsum(slab, axis=0) - slab

        def one_slice(packed):
            before_row, cells = packed
            lit = plane_in * jnp.exp(-extinction[:, None, None] * before_row[None])
            optical = 6.0 * cells / NZ
            depth_before = jnp.cumsum(optical, axis=0) - optical
            weight = jnp.exp(-depth_before) * (1.0 - jnp.exp(-optical))
            return jnp.sum(lit * weight[None], axis=1) * albedo[:, None]

        rows_out = lax.map(one_slice, (before, slab))
        leaving = plane_in * jnp.exp(-extinction[:, None, None] * jnp.sum(slab, axis=0)[None])
        return blur_plane(leaving, kernel), rows_out

    final_plane, rows_out = lax.scan(slab_step, lamp_plane, slabs)
    return rows_out.reshape(NL, C, NH).transpose(1, 0, 2)


def reference(density, active_list, light_dir, lamp_plane, extinction, blur_weights, albedo):
    kernel = (blur_weights / jnp.sum(blur_weights, axis=1, keepdims=True)).reshape(C, 5, 5)
    masked = density * live_cells(active_list)
    light_up = march(masked, lamp_plane, extinction, kernel, albedo)
    light_down = march(masked[::-1], lamp_plane, extinction, kernel, albedo)[:, ::-1, :]
    return jnp.where(light_dir[:, None, None] == 0, light_up, light_down)
```

```python
import jax
import jax.numpy as jnp
from jax import lax
from jax.experimental import pallas as pl
from jax.experimental.pallas import tpu as pltpu
from jax.sharding import PartitionSpec as P

MESH = pl.DeviceIdType.MESH
LOG2E = 1.4426950408889634
SLICES = 16
SLABS = 16
ROWS = 16
DEPTH = 32
WIDTH = 512
BLOCKS = WIDTH // 128
BRICK_ROWS = 8
EIGHTHS = 8
HALF = 4
BEFORE_MARCH = 2


def device(light, depth, height):
    return {"light": light, "depth": depth, "height": height}


def windows(block):
    lane = lax.broadcasted_iota(jnp.int32, (block.shape[0], 128), 1)
    parts = [block[:, 128 * m : 128 * m + 128] for m in range(BLOCKS)]
    near = [pltpu.roll(part, 32, 1) for part in parts]
    far = [pltpu.roll(part, 96, 1) for part in parts]
    made = [far[0]]
    for m in range(BLOCKS):
        made.append(near[m] if m == 0 else jnp.where(lane < 32, near[m - 1], near[m]))
        made.append(far[m] if m == BLOCKS - 1 else jnp.where(lane < 96, far[m], far[m + 1]))
    made.append(near[BLOCKS - 1])
    return made


def body(
    density, active, light_dir, lamp, extinction, blur_weights, albedo,
    out,
    dens, lampv, masked, wins, columns, edges, lampwin, lampbuf, lampedge, steps, leaving, planes, shade,
    load_sem, col_send, col_recv, up_send, down_send, edge_recv, mask_sem, lamp_sem, lampedge_sem, plane_sem,
):
    light, depth, height = (lax.axis_index(a) for a in ("light", "depth", "height"))
    heights = lax.axis_size("height")
    half, eighth = lax.div(light, EIGHTHS), lax.rem(light, EIGHTHS)
    sibling = 1 - depth
    has_below, has_above = height > 0, height < heights - 1
    low_edge = jnp.logical_and(eighth == 0, has_below)
    high_edge = jnp.logical_and(eighth == EIGHTHS - 1, has_above)
    mine = 2 * light + depth
    above, below = lax.rem(height + 1, heights), lax.rem(height + heights - 1, heights)
    first = HALF * half + 2 * depth

    chunk = SLICES // 4
    loads = [
        pltpu.make_async_copy(
            density.at[pl.ds(chunk * i, chunk)], dens.at[pl.ds(chunk * i, chunk)], load_sem.at[i]
        )
        for i in range(4)
    ]
    for load in loads:
        load.start()
    load_lamp = pltpu.make_async_copy(lamp.at[pl.ds(HALF * half, HALF)], lampv, load_sem.at[4])
    load_lamp.start()

    barrier = pltpu.get_barrier_semaphore()

    def greet(begin, at):
        @pl.loop(begin, 2 * SLABS)
        def _(j):
            other = lax.rem(mine + j, 2 * SLABS)
            pl.semaphore_signal(
                barrier,
                inc=1,
                device_id=device(lax.div(other, 2), lax.rem(other, 2), at),
                device_id_type=MESH,
            )

    greet(1, height)

    @pl.when(low_edge)
    def _():
        greet(0, below)

    @pl.when(high_edge)
    def _():
        greet(0, above)

    listed = active[...]
    live = []
    for m in range(BLOCKS):
        brick = light * (BLOCKS * heights) + height * BLOCKS + m
        found = jnp.max(jnp.where(listed == brick, 1.0, 0.0), axis=1, keepdims=True)
        live.append(
            jnp.concatenate(
                [jnp.broadcast_to(found[i : i + 1], (BRICK_ROWS, 128)) for i in range(2)], axis=0
            )
        )
    live = jnp.concatenate(live, axis=1)

    column = jnp.zeros((ROWS, WIDTH), jnp.float32)
    for i in range(4):
        loads[i].wait()
        for x in range(chunk * i, chunk * i + chunk):
            cells = dens[x] * live
            masked[depth, x] = cells
            column = column + cells
    for j, window in enumerate(windows(column)):
        wins[j] = window

    pl.semaphore_wait(
        barrier,
        2 * SLABS - 1 + 4 * has_below.astype(jnp.int32) + 4 * has_above.astype(jnp.int32),
    )

    @pl.loop(0, 2 * SLABS)
    def _(j):
        other = lax.rem(mine + j, 2 * SLABS)
        to = lax.div(other, 2)
        source = wins.at[lax.rem(to, EIGHTHS) + 1]

        @pl.when(j == 0)
        def _():
            pltpu.make_async_copy(source, columns.at[mine], col_recv).start()

        @pl.when(j > 0)
        def _():
            pltpu.make_async_remote_copy(
                source, columns.at[mine], col_send, col_recv,
                device_id=device(to, lax.rem(other, 2), height), device_id_type=MESH,
            ).start()

    @pl.when(has_above)
    def _():
        for j in range(4):
            pltpu.make_async_remote_copy(
                wins.at[EIGHTHS + 1], edges.at[mine], up_send, edge_recv,
                device_id=device(EIGHTHS * (j // 2), j % 2, above), device_id_type=MESH,
            ).start()

    @pl.when(has_below)
    def _():
        for j in range(4):
            pltpu.make_async_remote_copy(
                wins.at[0], edges.at[mine], down_send, edge_recv,
                device_id=device(EIGHTHS * (j // 2) + EIGHTHS - 1, j % 2, below), device_id_type=MESH,
            ).start()

    share = pltpu.make_async_remote_copy(
        masked.at[depth], masked.at[depth], mask_sem.at[0], mask_sem.at[1],
        device_id=device(light, sibling, height), device_id_type=MESH,
    )
    share.start()

    load_lamp.wait()
    for c in range(HALF):
        for j, window in enumerate(windows(lampv[c])):
            lampwin[j, c] = window
    share_lamp = pltpu.make_async_remote_copy(
        lampwin.at[eighth + 1, pl.ds(2 * sibling, 2)], lampbuf.at[depth], lamp_sem.at[0], lamp_sem.at[1],
        device_id=device(light, sibling, height), device_id_type=MESH,
    )
    share_lamp.start()
    lamp_up = jnp.logical_and(eighth == 0, has_above)
    lamp_down = jnp.logical_and(eighth == EIGHTHS - 1, has_below)

    def lamp_over(source, at):
        for to in range(2):
            pltpu.make_async_remote_copy(
                lampwin.at[source, pl.ds(2 * to, 2)], lampedge.at[depth], lampedge_sem.at[0], lampedge_sem.at[1],
                device_id=device(light, to, at), device_id_type=MESH,
            ).start()

    @pl.when(lamp_up)
    def _():
        lamp_over(EIGHTHS + 1, above)

    @pl.when(lamp_down)
    def _():
        lamp_over(0, below)

    lampbuf[depth] = lampwin[eighth + 1, pl.ds(2 * depth, 2)]

    lane = lax.broadcasted_iota(jnp.int32, (DEPTH, 128), 1)
    row = lax.broadcasted_iota(jnp.int32, (DEPTH, 128), 0)

    share.wait_recv()

    shown = [HALF * depth + i for i in range(HALF)]
    shown_down = [jnp.full((DEPTH, 128), light_dir[c], jnp.int32) == 1 for c in shown]
    shown_rate = [extinction[c] * -LOG2E for c in shown]

    def shading(m):
        lanes = pl.ds(pl.multiple_of(128 * m, 128), 128)

        def cells_of(x):
            return masked[:, x, :, lanes].reshape(DEPTH, 128)

        total = lax.fori_loop(
            0, SLICES, lambda x, t: t + cells_of(x), jnp.zeros((DEPTH, 128), jnp.float32), unroll=True
        )

        def one(x, running):
            cells = cells_of(x)
            after = running + cells
            behind = total - after
            optical = cells * (6.0 / DEPTH)
            summed = optical
            for step in (1, 2, 4, 8, 16):
                summed = summed + jnp.where(row >= step, pltpu.roll(summed, step, 0), 0.0)
            weight = jnp.exp(optical - summed) * (1.0 - jnp.exp(-optical))
            for i in range(HALF):
                before = jnp.where(shown_down[i], behind, running)
                shade[i, m, x] = jnp.exp2(before * shown_rate[i]) * weight
            return after

        def two(i, running):
            return one(2 * i + 1, one(2 * i, running))

        lax.fori_loop(0, SLICES // 2, two, jnp.zeros((DEPTH, 128), jnp.float32))

    @pl.loop(0, BEFORE_MARCH)
    def _(m):
        shading(m)

    pltpu.make_async_copy(columns, columns, col_recv).wait()
    share_lamp.wait_recv()

    @pl.when(jnp.logical_or(low_edge, high_edge))
    def _():
        pltpu.make_async_copy(edges, edges, edge_recv).wait()
        pltpu.make_async_copy(lampedge, lampedge, lampedge_sem.at[1]).wait()

    foreign = jnp.logical_or(
        lane < jnp.where(low_edge, 32, 0), lane >= jnp.where(high_edge, 96, 128)
    )
    inside = jnp.logical_and(
        lane >= jnp.where(jnp.logical_and(eighth == 0, height == 0), 32, 0),
        lane < jnp.where(jnp.logical_and(eighth == EIGHTHS - 1, height == heights - 1), 96, 128),
    )
    down = [jnp.full((DEPTH, 128), light_dir[first + i], jnp.int32) == 1 for i in range(2)]
    rate = [extinction[first + i] * -LOG2E for i in range(2)]
    scale = []
    for i in range(2):
        whole = blur_weights[first + i, 0]
        for t in range(1, 25):
            whole = whole + blur_weights[first + i, t]
        scale.append(jnp.where(inside, 1.0 / jnp.full((DEPTH, 128), whole, jnp.float32), 0.0))

    def column_of(k):
        own = columns[pl.ds(2 * k, 2)].reshape(DEPTH, 128)
        return jnp.where(foreign, edges[pl.ds(2 * k, 2)].reshape(DEPTH, 128), own)

    def factors(s):
        ahead, back = column_of(s), column_of(SLABS - 1 - s)
        return tuple(
            jnp.exp2(jnp.where(down[i], back, ahead) * rate[i]) * scale[i] for i in range(2)
        )

    def blurred(plane, i):
        moved = [plane if b == 0 else pltpu.roll(plane, (-b) % 128, 1) for b in range(-2, 3)]
        total = None
        for a in range(-2, 3):
            term = None
            for b in range(5):
                part = moved[b] * blur_weights[first + i, 5 * (a + 2) + b]
                term = part if term is None else term + part
            if a:
                term = pltpu.roll(term, (-a) % DEPTH, 0)
                term = jnp.where(row >= -a if a < 0 else row < DEPTH - a, term, 0.0)
            total = term if total is None else total + term
        return total

    def advance(s, carry):
        plane, factor = carry
        later = factors(s + 1)
        plane = tuple(blurred(plane[i] * factor[i], i) for i in range(2))
        for i in range(2):
            steps[i, s + 1] = plane[i]
        return plane, later

    start = []
    for i in range(2):
        own = jnp.concatenate([lampbuf[0, i], lampbuf[1, i]], axis=0)
        other = jnp.concatenate([lampedge[0, i], lampedge[1, i]], axis=0)
        start.append(jnp.where(foreign, other, own))
        steps[i, 0] = start[i]
    carry = lax.fori_loop(0, SLABS // 2 - 1, advance, (tuple(start), factors(0)))

    def send(k):
        alone = jnp.logical_and(k == light, half == depth)
        to = planes.at[depth * EIGHTHS + eighth]

        @pl.when(alone)
        def _():
            pltpu.make_async_copy(leaving.at[k], to, plane_sem.at[1]).start()

        @pl.when(jnp.logical_not(alone))
        def _():
            pltpu.make_async_remote_copy(
                leaving.at[k], to, plane_sem.at[0], plane_sem.at[1],
                device_id=device(k, half, height), device_id_type=MESH,
            ).start()

    def advance_and_send(j, carry):
        s = j + SLABS // 2 - 1
        carry = advance(s, carry)
        late = carry[0]
        early = [steps[i, SLABS - 2 - s] for i in range(2)]
        front = [jnp.where(down[i], early[i], late[i]) for i in range(2)]
        rear = [jnp.where(down[i], late[i], early[i]) for i in range(2)]
        for k, pair in ((s + 1, front), (SLABS - 2 - s, rear)):
            leaving[k] = jnp.where(lane < 64, pltpu.roll(pair[0], 96, 1), pltpu.roll(pair[1], 32, 1))
            send(k)
        return carry

    lax.fori_loop(0, SLABS // 2, advance_and_send, carry)

    @pl.loop(BEFORE_MARCH, BLOCKS)
    def _(m):
        shading(m)

    pltpu.make_async_copy(planes, planes, plane_sem.at[1]).wait()

    for m in range(BLOCKS):
        lanes = pl.ds(128 * m, 128)
        for pair in range(2):
            even, odd = planes[EIGHTHS * pair + 2 * m], planes[EIGHTHS * pair + 2 * m + 1]
            entering = (
                jnp.where(lane < 64, even, pltpu.roll(odd, 64, 1)),
                jnp.where(lane < 64, pltpu.roll(even, 64, 1), odd),
            )
            for i in range(2):
                c = 2 * pair + i
                seen = jnp.sum(shade[c, m] * entering[i][None], axis=1)
                out[c, :, lanes] = seen * albedo[HALF * depth + c]

    pltpu.make_async_copy(
        columns.at[pl.ds(0, 2 * SLABS - 1)], columns.at[pl.ds(0, 2 * SLABS - 1)], col_send
    ).wait()

    @pl.when(has_above)
    def _():
        pltpu.make_async_copy(wins.at[pl.ds(0, 4)], wins.at[pl.ds(0, 4)], up_send).wait()

    @pl.when(has_below)
    def _():
        pltpu.make_async_copy(wins.at[pl.ds(0, 4)], wins.at[pl.ds(0, 4)], down_send).wait()

    share.wait_send()
    share_lamp.wait_send()

    @pl.when(jnp.logical_or(lamp_up, lamp_down))
    def _():
        pltpu.make_async_copy(lampedge, lampedge, lampedge_sem.at[0]).wait()

    @pl.when(half == depth)
    def _():
        part = leaving.at[pl.ds(0, SLABS - 1)]
        pltpu.make_async_copy(part, part, plane_sem.at[0]).wait()

    @pl.when(half != depth)
    def _():
        pltpu.make_async_copy(leaving, leaving, plane_sem.at[0]).wait()


def local(density, active_list, light_dir, lamp_plane, extinction, blur_weights, albedo):
    f32 = jnp.float32
    vmem = pl.BlockSpec(memory_space=pltpu.VMEM)
    smem = pl.BlockSpec(memory_space=pltpu.SMEM)
    anywhere = pl.BlockSpec(memory_space=pl.ANY)
    dma = pltpu.SemaphoreType.DMA
    return pl.pallas_call(
        body,
        out_shape=jax.ShapeDtypeStruct((HALF, SLICES, WIDTH), f32),
        in_specs=[anywhere, vmem, smem, anywhere, smem, smem, smem],
        out_specs=vmem,
        scratch_shapes=[
            pltpu.VMEM((SLICES, ROWS, WIDTH), f32),
            pltpu.VMEM((HALF, ROWS, WIDTH), f32),
            pltpu.VMEM((2, SLICES, ROWS, WIDTH), f32),
            pltpu.VMEM((EIGHTHS + 2, ROWS, 128), f32),
            pltpu.VMEM((2 * SLABS, ROWS, 128), f32),
            pltpu.VMEM((2 * SLABS, ROWS, 128), f32),
            pltpu.VMEM((EIGHTHS + 2, HALF, ROWS, 128), f32),
            pltpu.VMEM((2, 2, ROWS, 128), f32),
            pltpu.VMEM((2, 2, ROWS, 128), f32),
            pltpu.VMEM((2, SLABS, DEPTH, 128), f32),
            pltpu.VMEM((SLABS, DEPTH, 128), f32),
            pltpu.VMEM((2 * EIGHTHS, DEPTH, 128), f32),
            pltpu.VMEM((HALF, BLOCKS, SLICES, DEPTH, 128), f32),
            dma((5,)), dma(()), dma(()), dma(()), dma(()), dma(()), dma((2,)), dma((2,)), dma((2,)), dma((2,)),
        ],
        compiler_params=pltpu.CompilerParams(
            collective_id=0, has_side_effects=True, vmem_limit_bytes=40 * 1024 * 1024
        ),
        name="march_and_shade",
    )(density, active_list, light_dir, lamp_plane, extinction, blur_weights, albedo)


def solution(mesh):
    in_specs = (
        P("light", "depth", "height"),
        P("depth", None),
        P(),
        P(None, "depth", "height"),
        P(),
        P(),
        P(),
    )
    out_specs = P("depth", "light", "height")
    return jax.shard_map(local, mesh=mesh, in_specs=in_specs, out_specs=out_specs, check_vma=False)
```

```python
import jax
import jax.numpy as jnp
from jax import lax
from jax.experimental import pallas as pl
from jax.experimental.pallas import tpu as pltpu
from jax.sharding import PartitionSpec as P

MESH = pl.DeviceIdType.MESH
LOG2E = 1.4426950408889634
SLICES = 16
SLABS = 16
ROWS = 16
DEPTH = 32
WIDTH = 512
BLOCKS = WIDTH // 128
BRICK_ROWS = 8
EIGHTHS = 8
HALF = 4
BEFORE_MARCH = 2


def device(light, depth, height):
    return {"light": light, "depth": depth, "height": height}


def windows(block):
    lane = lax.broadcasted_iota(jnp.int32, (block.shape[0], 128), 1)
    parts = [block[:, 128 * m : 128 * m + 128] for m in range(BLOCKS)]
    near = [pltpu.roll(part, 32, 1) for part in parts]
    far = [pltpu.roll(part, 96, 1) for part in parts]
    made = [far[0]]
    for m in range(BLOCKS):
        made.append(near[m] if m == 0 else jnp.where(lane < 32, near[m - 1], near[m]))
        made.append(far[m] if m == BLOCKS - 1 else jnp.where(lane < 96, far[m], far[m + 1]))
    made.append(near[BLOCKS - 1])
    return made


def body(
    density, active_hbm, light_dir_hbm, lamp, extinction_hbm, blur_hbm, albedo_hbm,
    out,
    active, light_dir, extinction, blur_weights, albedo, dens, lampv, masked, wins, columns, edges, lampwin, lampbuf, lampedge, steps, leaving, planes, shade,
    load_sem, col_send, col_recv, up_send, down_send, edge_recv, mask_sem, lamp_sem, lampedge_sem, plane_sem,
):
    light, depth, height = (lax.axis_index(a) for a in ("light", "depth", "height"))
    heights = lax.axis_size("height")
    half, eighth = lax.div(light, EIGHTHS), lax.rem(light, EIGHTHS)
    sibling = 1 - depth
    has_below, has_above = height > 0, height < heights - 1
    low_edge = jnp.logical_and(eighth == 0, has_below)
    high_edge = jnp.logical_and(eighth == EIGHTHS - 1, has_above)
    mine = 2 * light + depth
    above, below = lax.rem(height + 1, heights), lax.rem(height + heights - 1, heights)
    first = HALF * half + 2 * depth

    chunk = SLICES // 4
    loads = [
        pltpu.make_async_copy(
            density.at[pl.ds(chunk * i, chunk)], dens.at[pl.ds(chunk * i, chunk)], load_sem.at[i]
        )
        for i in range(4)
    ]
    for load in loads:
        load.start()
    load_lamp = pltpu.make_async_copy(lamp.at[pl.ds(HALF * half, HALF)], lampv, load_sem.at[4])
    load_lamp.start()
    load_active = pltpu.make_async_copy(active_hbm, active, load_sem.at[5])
    load_small = [
        pltpu.make_async_copy(light_dir_hbm, light_dir, load_sem.at[6]),
        pltpu.make_async_copy(extinction_hbm, extinction, load_sem.at[7]),
        pltpu.make_async_copy(blur_hbm, blur_weights, load_sem.at[8]),
        pltpu.make_async_copy(albedo_hbm, albedo, load_sem.at[9]),
    ]
    load_active.start()
    for load in load_small:
        load.start()

    barrier = pltpu.get_barrier_semaphore()

    def greet(begin, at):
        @pl.loop(begin, 2 * SLABS)
        def _(j):
            other = lax.rem(mine + j, 2 * SLABS)
            pl.semaphore_signal(
                barrier,
                inc=1,
                device_id=device(lax.div(other, 2), lax.rem(other, 2), at),
                device_id_type=MESH,
            )

    greet(1, height)

    @pl.when(low_edge)
    def _():
        greet(0, below)

    @pl.when(high_edge)
    def _():
        greet(0, above)

    load_active.wait()
    listed = active[...]
    live = []
    for m in range(BLOCKS):
        brick = light * (BLOCKS * heights) + height * BLOCKS + m
        found = jnp.max(jnp.where(listed == brick, 1.0, 0.0), axis=1, keepdims=True)
        live.append(
            jnp.concatenate(
                [jnp.broadcast_to(found[i : i + 1], (BRICK_ROWS, 128)) for i in range(2)], axis=0
            )
        )
    live = jnp.concatenate(live, axis=1)

    column = jnp.zeros((ROWS, WIDTH), jnp.float32)
    for i in range(4):
        loads[i].wait()
        for x in range(chunk * i, chunk * i + chunk):
            cells = dens[x] * live
            masked[depth, x] = cells
            column = column + cells
    for j, window in enumerate(windows(column)):
        wins[j] = window

    pl.semaphore_wait(
        barrier,
        2 * SLABS - 1 + 4 * has_below.astype(jnp.int32) + 4 * has_above.astype(jnp.int32),
    )

    @pl.loop(0, 2 * SLABS)
    def _(j):
        other = lax.rem(mine + j, 2 * SLABS)
        to = lax.div(other, 2)
        source = wins.at[lax.rem(to, EIGHTHS) + 1]

        @pl.when(j == 0)
        def _():
            pltpu.make_async_copy(source, columns.at[mine], col_recv).start()

        @pl.when(j > 0)
        def _():
            pltpu.make_async_remote_copy(
                source, columns.at[mine], col_send, col_recv,
                device_id=device(to, lax.rem(other, 2), height), device_id_type=MESH,
            ).start()

    @pl.when(has_above)
    def _():
        for j in range(4):
            pltpu.make_async_remote_copy(
                wins.at[EIGHTHS + 1], edges.at[mine], up_send, edge_recv,
                device_id=device(EIGHTHS * (j // 2), j % 2, above), device_id_type=MESH,
            ).start()

    @pl.when(has_below)
    def _():
        for j in range(4):
            pltpu.make_async_remote_copy(
                wins.at[0], edges.at[mine], down_send, edge_recv,
                device_id=device(EIGHTHS * (j // 2) + EIGHTHS - 1, j % 2, below), device_id_type=MESH,
            ).start()

    share = pltpu.make_async_remote_copy(
        masked.at[depth], masked.at[depth], mask_sem.at[0], mask_sem.at[1],
        device_id=device(light, sibling, height), device_id_type=MESH,
    )
    share.start()

    load_lamp.wait()
    for c in range(HALF):
        for j, window in enumerate(windows(lampv[c])):
            lampwin[j, c] = window
    share_lamp = pltpu.make_async_remote_copy(
        lampwin.at[eighth + 1, pl.ds(2 * sibling, 2)], lampbuf.at[depth], lamp_sem.at[0], lamp_sem.at[1],
        device_id=device(light, sibling, height), device_id_type=MESH,
    )
    share_lamp.start()
    lamp_up = jnp.logical_and(eighth == 0, has_above)
    lamp_down = jnp.logical_and(eighth == EIGHTHS - 1, has_below)

    def lamp_over(source, at):
        for to in range(2):
            pltpu.make_async_remote_copy(
                lampwin.at[source, pl.ds(2 * to, 2)], lampedge.at[depth], lampedge_sem.at[0], lampedge_sem.at[1],
                device_id=device(light, to, at), device_id_type=MESH,
            ).start()

    @pl.when(lamp_up)
    def _():
        lamp_over(EIGHTHS + 1, above)

    @pl.when(lamp_down)
    def _():
        lamp_over(0, below)

    lampbuf[depth] = lampwin[eighth + 1, pl.ds(2 * depth, 2)]

    lane = lax.broadcasted_iota(jnp.int32, (DEPTH, 128), 1)
    row = lax.broadcasted_iota(jnp.int32, (DEPTH, 128), 0)

    share.wait_recv()

    for load in load_small:
        load.wait()
    shown = [HALF * depth + i for i in range(HALF)]
    shown_down = [jnp.full((DEPTH, 128), light_dir[c], jnp.int32) == 1 for c in shown]
    shown_rate = [extinction[c] * -LOG2E for c in shown]

    def shading(m):
        lanes = pl.ds(pl.multiple_of(128 * m, 128), 128)

        def cells_of(x):
            return masked[:, x, :, lanes].reshape(DEPTH, 128)

        total = lax.fori_loop(
            0, SLICES, lambda x, t: t + cells_of(x), jnp.zeros((DEPTH, 128), jnp.float32), unroll=True
        )

        def one(x, running):
            cells = cells_of(x)
            after = running + cells
            behind = total - after
            optical = cells * (6.0 / DEPTH)
            summed = optical
            for step in (1, 2, 4, 8, 16):
                summed = summed + jnp.where(row >= step, pltpu.roll(summed, step, 0), 0.0)
            weight = jnp.exp(optical - summed) * (1.0 - jnp.exp(-optical))
            for i in range(HALF):
                before = jnp.where(shown_down[i], behind, running)
                shade[i, m, x] = jnp.exp2(before * shown_rate[i]) * weight
            return after

        def two(i, running):
            return one(2 * i + 1, one(2 * i, running))

        lax.fori_loop(0, SLICES // 2, two, jnp.zeros((DEPTH, 128), jnp.float32))

    @pl.loop(0, BEFORE_MARCH)
    def _(m):
        shading(m)

    pltpu.make_async_copy(columns, columns, col_recv).wait()
    share_lamp.wait_recv()

    @pl.when(jnp.logical_or(low_edge, high_edge))
    def _():
        pltpu.make_async_copy(edges, edges, edge_recv).wait()
        pltpu.make_async_copy(lampedge, lampedge, lampedge_sem.at[1]).wait()

    foreign = jnp.logical_or(
        lane < jnp.where(low_edge, 32, 0), lane >= jnp.where(high_edge, 96, 128)
    )
    inside = jnp.logical_and(
        lane >= jnp.where(jnp.logical_and(eighth == 0, height == 0), 32, 0),
        lane < jnp.where(jnp.logical_and(eighth == EIGHTHS - 1, height == heights - 1), 96, 128),
    )
    down = [jnp.full((DEPTH, 128), light_dir[first + i], jnp.int32) == 1 for i in range(2)]
    rate = [extinction[first + i] * -LOG2E for i in range(2)]
    scale = []
    for i in range(2):
        whole = blur_weights[first + i, 0]
        for t in range(1, 25):
            whole = whole + blur_weights[first + i, t]
        scale.append(jnp.where(inside, 1.0 / jnp.full((DEPTH, 128), whole, jnp.float32), 0.0))

    def column_of(k):
        own = columns[pl.ds(2 * k, 2)].reshape(DEPTH, 128)
        return jnp.where(foreign, edges[pl.ds(2 * k, 2)].reshape(DEPTH, 128), own)

    def factors(s):
        ahead, back = column_of(s), column_of(SLABS - 1 - s)
        return tuple(
            jnp.exp2(jnp.where(down[i], back, ahead) * rate[i]) * scale[i] for i in range(2)
        )

    def blurred(plane, i):
        moved = [plane if b == 0 else pltpu.roll(plane, (-b) % 128, 1) for b in range(-2, 3)]
        total = None
        for a in range(-2, 3):
            term = None
            for b in range(5):
                part = moved[b] * blur_weights[first + i, 5 * (a + 2) + b]
                term = part if term is None else term + part
            if a:
                term = pltpu.roll(term, (-a) % DEPTH, 0)
                term = jnp.where(row >= -a if a < 0 else row < DEPTH - a, term, 0.0)
            total = term if total is None else total + term
        return total

    def advance(s, carry):
        plane, factor = carry
        later = factors(s + 1)
        plane = tuple(blurred(plane[i] * factor[i], i) for i in range(2))
        for i in range(2):
            steps[i, s + 1] = plane[i]
        return plane, later

    start = []
    for i in range(2):
        own = jnp.concatenate([lampbuf[0, i], lampbuf[1, i]], axis=0)
        other = jnp.concatenate([lampedge[0, i], lampedge[1, i]], axis=0)
        start.append(jnp.where(foreign, other, own))
        steps[i, 0] = start[i]
    carry = lax.fori_loop(0, SLABS // 2 - 1, advance, (tuple(start), factors(0)))

    def send(k):
        alone = jnp.logical_and(k == light, half == depth)
        to = planes.at[depth * EIGHTHS + eighth]

        @pl.when(alone)
        def _():
            pltpu.make_async_copy(leaving.at[k], to, plane_sem.at[1]).start()

        @pl.when(jnp.logical_not(alone))
        def _():
            pltpu.make_async_remote_copy(
                leaving.at[k], to, plane_sem.at[0], plane_sem.at[1],
                device_id=device(k, half, height), device_id_type=MESH,
            ).start()

    def advance_and_send(j, carry):
        s = j + SLABS // 2 - 1
        carry = advance(s, carry)
        late = carry[0]
        early = [steps[i, SLABS - 2 - s] for i in range(2)]
        front = [jnp.where(down[i], early[i], late[i]) for i in range(2)]
        rear = [jnp.where(down[i], late[i], early[i]) for i in range(2)]
        for k, pair in ((s + 1, front), (SLABS - 2 - s, rear)):
            leaving[k] = jnp.where(lane < 64, pltpu.roll(pair[0], 96, 1), pltpu.roll(pair[1], 32, 1))
            send(k)
        return carry

    lax.fori_loop(0, SLABS // 2, advance_and_send, carry)

    @pl.loop(BEFORE_MARCH, BLOCKS)
    def _(m):
        shading(m)

    pltpu.make_async_copy(planes, planes, plane_sem.at[1]).wait()

    for m in range(BLOCKS):
        lanes = pl.ds(128 * m, 128)
        for pair in range(2):
            even, odd = planes[EIGHTHS * pair + 2 * m], planes[EIGHTHS * pair + 2 * m + 1]
            entering = (
                jnp.where(lane < 64, even, pltpu.roll(odd, 64, 1)),
                jnp.where(lane < 64, pltpu.roll(even, 64, 1), odd),
            )
            for i in range(2):
                c = 2 * pair + i
                seen = jnp.sum(shade[c, m] * entering[i][None], axis=1)
                out[c, :, lanes] = seen * albedo[HALF * depth + c]

    pltpu.make_async_copy(
        columns.at[pl.ds(0, 2 * SLABS - 1)], columns.at[pl.ds(0, 2 * SLABS - 1)], col_send
    ).wait()

    @pl.when(has_above)
    def _():
        pltpu.make_async_copy(wins.at[pl.ds(0, 4)], wins.at[pl.ds(0, 4)], up_send).wait()

    @pl.when(has_below)
    def _():
        pltpu.make_async_copy(wins.at[pl.ds(0, 4)], wins.at[pl.ds(0, 4)], down_send).wait()

    share.wait_send()
    share_lamp.wait_send()

    @pl.when(jnp.logical_or(lamp_up, lamp_down))
    def _():
        pltpu.make_async_copy(lampedge, lampedge, lampedge_sem.at[0]).wait()

    @pl.when(half == depth)
    def _():
        part = leaving.at[pl.ds(0, SLABS - 1)]
        pltpu.make_async_copy(part, part, plane_sem.at[0]).wait()

    @pl.when(half != depth)
    def _():
        pltpu.make_async_copy(leaving, leaving, plane_sem.at[0]).wait()


def local(density, active_list, light_dir, lamp_plane, extinction, blur_weights, albedo):
    f32 = jnp.float32
    vmem = pl.BlockSpec(memory_space=pltpu.VMEM)
    anywhere = pl.BlockSpec(memory_space=pl.ANY)
    dma = pltpu.SemaphoreType.DMA
    return pl.pallas_call(
        body,
        out_shape=jax.ShapeDtypeStruct((HALF, SLICES, WIDTH), f32),
        in_specs=[anywhere] * 7,
        out_specs=vmem,
        scratch_shapes=[
            pltpu.VMEM(active_list.shape, jnp.int32),
            pltpu.SMEM(light_dir.shape, jnp.int32),
            pltpu.SMEM(extinction.shape, f32),
            pltpu.SMEM(blur_weights.shape, f32),
            pltpu.SMEM(albedo.shape, f32),
            pltpu.VMEM((SLICES, ROWS, WIDTH), f32),
            pltpu.VMEM((HALF, ROWS, WIDTH), f32),
            pltpu.VMEM((2, SLICES, ROWS, WIDTH), f32),
            pltpu.VMEM((EIGHTHS + 2, ROWS, 128), f32),
            pltpu.VMEM((2 * SLABS, ROWS, 128), f32),
            pltpu.VMEM((2 * SLABS, ROWS, 128), f32),
            pltpu.VMEM((EIGHTHS + 2, HALF, ROWS, 128), f32),
            pltpu.VMEM((2, 2, ROWS, 128), f32),
            pltpu.VMEM((2, 2, ROWS, 128), f32),
            pltpu.VMEM((2, SLABS, DEPTH, 128), f32),
            pltpu.VMEM((SLABS, DEPTH, 128), f32),
            pltpu.VMEM((2 * EIGHTHS, DEPTH, 128), f32),
            pltpu.VMEM((HALF, BLOCKS, SLICES, DEPTH, 128), f32),
            dma((10,)), dma(()), dma(()), dma(()), dma(()), dma(()), dma((2,)), dma((2,)), dma((2,)), dma((2,)),
        ],
        compiler_params=pltpu.CompilerParams(
            collective_id=0, has_side_effects=True, vmem_limit_bytes=63 * 1024 * 1024
        ),
        name="march_and_shade",
    )(density, active_list, light_dir, lamp_plane, extinction, blur_weights, albedo)


def solution(mesh):
    in_specs = (
        P("light", "depth", "height"),
        P("depth", None),
        P(),
        P(None, "depth", "height"),
        P(),
        P(),
        P(),
    )
    out_specs = P("depth", "light", "height")
    return jax.shard_map(local, mesh=mesh, in_specs=in_specs, out_specs=out_specs, check_vma=False)
```

```python
import jax
import jax.numpy as jnp
from jax import lax
from jax.experimental import pallas as pl
from jax.experimental.pallas import tpu as pltpu
from jax.sharding import PartitionSpec as P

MESH = pl.DeviceIdType.MESH
LOG2E = 1.4426950408889634
SLICES = 16
SLABS = 16
ROWS = 16
DEPTH = 32
WIDTH = 512
BLOCKS = WIDTH // 128
BRICK_ROWS = 8
EIGHTHS = 8
HALF = 4
BEFORE_RELAY = 1
BEFORE_MARCH = 2
SIDE = 4


def hops(down, right):
    return min(down, SIDE - down) + min(right, SIDE - right)


OTHERS = sorted(
    ((down, right) for down in range(SIDE) for right in range(SIDE) if down or right),
    key=lambda step: -hops(*step),
)
FAR = [step for step in OTHERS if hops(*step) > 2]
NEAR = [step for step in OTHERS if hops(*step) <= 2]


def chip_at(light, step):
    down = lax.rem(lax.div(light, SIDE) + step[0], SIDE)
    return SIDE * down + lax.rem(lax.rem(light, SIDE) + step[1], SIDE)


def hops_between(one, other):
    total = 0
    for a, b in (
        (lax.div(one, SIDE), lax.div(other, SIDE)),
        (lax.rem(one, SIDE), lax.rem(other, SIDE)),
    ):
        way = lax.rem(a - b + SIDE, SIDE)
        total = total + jnp.minimum(way, SIDE - way)
    return total


def device(light, depth, height):
    return {"light": light, "depth": depth, "height": height}


def windows(block):
    lane = lax.broadcasted_iota(jnp.int32, (block.shape[0], 128), 1)
    parts = [block[:, 128 * m : 128 * m + 128] for m in range(BLOCKS)]
    near = [pltpu.roll(part, 32, 1) for part in parts]
    far = [pltpu.roll(part, 96, 1) for part in parts]
    made = [far[0]]
    for m in range(BLOCKS):
        made.append(near[m] if m == 0 else jnp.where(lane < 32, near[m - 1], near[m]))
        made.append(far[m] if m == BLOCKS - 1 else jnp.where(lane < 96, far[m], far[m + 1]))
    made.append(near[BLOCKS - 1])
    return made


def packed_low(window):
    lane = lax.broadcasted_iota(jnp.int32, (8, 128), 1)
    return jnp.where(lane < 32, window[:8], pltpu.roll(window[8:], 32, 1))


def packed_high(window):
    lane = lax.broadcasted_iota(jnp.int32, (8, 128), 1)
    return jnp.where(lane >= 96, window[:8], pltpu.roll(window[8:], 96, 1))


def body(
    density, active_hbm, light_dir_hbm, lamp, extinction_hbm, blur_hbm, albedo_hbm,
    out,
    active, light_dir, extinction, blur_weights, albedo, dens, lampv, masked, wins, rims, columns, packed, edges, lampwin, lamprim, lampbuf, lampedge, steps, leaving, planes, shade, taps,
    load_sem, col_send, far_recv, near_recv, relay_sem, up_send, down_send, rim_recv, rim_sem, mask_sem, lamp_sem, lampedge_sem, plane_sem,
):
    light, depth, height = (lax.axis_index(a) for a in ("light", "depth", "height"))
    heights = lax.axis_size("height")
    half, eighth = lax.div(light, EIGHTHS), lax.rem(light, EIGHTHS)
    sibling = 1 - depth
    has_below, has_above = height > 0, height < heights - 1
    low_edge = jnp.logical_and(eighth == 0, has_below)
    high_edge = jnp.logical_and(eighth == EIGHTHS - 1, has_above)
    mine = 2 * light + depth
    above, below = lax.rem(height + 1, heights), lax.rem(height + heights - 1, heights)
    first = HALF * half + 2 * depth

    chunk = SLICES // 4
    loads = [
        pltpu.make_async_copy(
            density.at[pl.ds(chunk * i, chunk)], dens.at[pl.ds(chunk * i, chunk)], load_sem.at[i]
        )
        for i in range(4)
    ]
    for load in loads:
        load.start()
    barrier = pltpu.get_barrier_semaphore()

    def greet(to, core, at):
        pl.semaphore_signal(barrier, inc=1, device_id=device(to, core, at), device_id_type=MESH)

    def greet_group(at):
        @pl.loop(0, 2 * SLABS)
        def _(j):
            other = lax.rem(mine + SLABS + j, 2 * SLABS)
            greet(lax.div(other, 2), lax.rem(other, 2), at)

    for step in FAR:
        for core in range(2):
            greet(chip_at(light, step), core, height)

    @pl.when(low_edge)
    def _():
        greet_group(below)

    @pl.when(high_edge)
    def _():
        greet_group(above)

    for step in NEAR:
        for core in range(2):
            greet(chip_at(light, step), core, height)
    greet(light, sibling, height)

    load_lamp = pltpu.make_async_copy(lamp.at[pl.ds(HALF * half, HALF)], lampv, load_sem.at[4])
    load_lamp.start()
    load_active = pltpu.make_async_copy(active_hbm, active, load_sem.at[5])
    load_small = [
        pltpu.make_async_copy(light_dir_hbm, light_dir, load_sem.at[6]),
        pltpu.make_async_copy(extinction_hbm, extinction, load_sem.at[7]),
        pltpu.make_async_copy(blur_hbm, blur_weights, load_sem.at[8]),
        pltpu.make_async_copy(albedo_hbm, albedo, load_sem.at[9]),
    ]
    load_active.start()
    for load in load_small:
        load.start()

    load_active.wait()
    listed = active[...]
    live = []
    for m in range(BLOCKS):
        brick = light * (BLOCKS * heights) + height * BLOCKS + m
        found = jnp.max(jnp.where(listed == brick, 1.0, 0.0), axis=1, keepdims=True)
        live.append(
            jnp.concatenate(
                [jnp.broadcast_to(found[i : i + 1], (BRICK_ROWS, 128)) for i in range(2)], axis=0
            )
        )
    live = jnp.concatenate(live, axis=1)

    column = jnp.zeros((ROWS, WIDTH), jnp.float32)
    for i in range(4):
        loads[i].wait()
        for x in range(chunk * i, chunk * i + chunk):
            cells = dens[x] * live
            masked[depth, x] = cells
            column = column + cells
    made = windows(column)
    for j in range(EIGHTHS):
        wins[j] = made[j + 1]
    rims[0] = packed_high(made[0])
    rims[1] = packed_low(made[-1])

    pl.semaphore_wait(
        barrier,
        2 * SLABS - 1 + 4 * has_below.astype(jnp.int32) + 4 * has_above.astype(jnp.int32),
    )

    def send_rim(side, to, at, left):
        pltpu.make_async_remote_copy(
            rims.at[side], packed.at[depth, light], left, rim_recv,
            device_id=device(to, depth, at), device_id_type=MESH,
        ).start()

    @pl.when(has_above)
    def _():
        for to in (0, EIGHTHS):
            send_rim(1, to, above, up_send)

    @pl.when(has_below)
    def _():
        for to in (EIGHTHS - 1, SLABS - 1):
            send_rim(0, to, below, down_send)

    def send_window(to, core, arrived):
        pltpu.make_async_remote_copy(
            wins.at[lax.rem(to, EIGHTHS)], columns.at[mine], col_send, arrived,
            device_id=device(to, core, height), device_id_type=MESH,
        ).start()

    for step in FAR:
        for core in range(2):
            send_window(chip_at(light, step), core, far_recv)
    for step in NEAR:
        send_window(chip_at(light, step), depth, near_recv)

    def relay(block, source):
        pltpu.make_async_remote_copy(
            source, columns.at[block], relay_sem.at[0], relay_sem.at[1],
            device_id=device(light, sibling, height), device_id_type=MESH,
        ).start()

    relay(mine, wins.at[eighth])
    columns[mine] = wins[eighth]

    share = pltpu.make_async_remote_copy(
        masked.at[depth], masked.at[depth], mask_sem.at[0], mask_sem.at[1],
        device_id=device(light, sibling, height), device_id_type=MESH,
    )
    share.start()

    load_lamp.wait()
    for c in range(HALF):
        made = windows(lampv[c])
        for j in range(EIGHTHS):
            lampwin[j, c] = made[j + 1]
        lamprim[0, c] = packed_high(made[0])
        lamprim[1, c] = packed_low(made[-1])
    share_lamp = pltpu.make_async_remote_copy(
        lampwin.at[eighth, pl.ds(2 * sibling, 2)], lampbuf.at[depth], lamp_sem.at[0], lamp_sem.at[1],
        device_id=device(light, sibling, height), device_id_type=MESH,
    )
    share_lamp.start()
    lamp_up = jnp.logical_and(eighth == 0, has_above)
    lamp_down = jnp.logical_and(eighth == EIGHTHS - 1, has_below)

    def lamp_over(source, at):
        for to in range(2):
            pltpu.make_async_remote_copy(
                lamprim.at[source, pl.ds(2 * to, 2)], lampedge.at[depth], lampedge_sem.at[0], lampedge_sem.at[1],
                device_id=device(light, to, at), device_id_type=MESH,
            ).start()

    @pl.when(lamp_up)
    def _():
        lamp_over(1, above)

    @pl.when(lamp_down)
    def _():
        lamp_over(0, below)

    lampbuf[depth] = lampwin[eighth, pl.ds(2 * depth, 2)]

    lane = lax.broadcasted_iota(jnp.int32, (DEPTH, 128), 1)
    row = lax.broadcasted_iota(jnp.int32, (DEPTH, 128), 0)

    share.wait_recv()

    for load in load_small:
        load.wait()
    shown = [HALF * depth + i for i in range(HALF)]
    shown_down = [jnp.full((DEPTH, 128), light_dir[c], jnp.int32) == 1 for c in shown]
    shown_rate = [extinction[c] * -LOG2E for c in shown]

    def shading(m):
        lanes = pl.ds(pl.multiple_of(128 * m, 128), 128)

        def cells_of(x):
            return masked[:, x, :, lanes].reshape(DEPTH, 128)

        total = lax.fori_loop(
            0, SLICES, lambda x, t: t + cells_of(x), jnp.zeros((DEPTH, 128), jnp.float32), unroll=True
        )

        def one(x, running):
            cells = cells_of(x)
            after = running + cells
            behind = total - after
            optical = cells * (6.0 / DEPTH)
            summed = optical
            for step in (1, 2, 4, 8, 16):
                summed = summed + jnp.where(row >= step, pltpu.roll(summed, step, 0), 0.0)
            weight = jnp.exp(optical - summed) * (1.0 - jnp.exp(-optical))
            for i in range(HALF):
                before = jnp.where(shown_down[i], behind, running)
                shade[i, m, x] = jnp.exp2(before * shown_rate[i]) * weight
            return after

        def two(i, running):
            return one(2 * i + 1, one(2 * i, running))

        lax.fori_loop(0, SLICES // 2, two, jnp.zeros((DEPTH, 128), jnp.float32))

    for i in range(2):
        for t in range(25):
            taps[i, t] = jnp.full((8, 128), blur_weights[first + i, t], jnp.float32)

    @pl.loop(0, BEFORE_RELAY)
    def _(m):
        shading(m)

    pltpu.make_async_copy(
        columns.at[pl.ds(0, len(NEAR))], columns.at[pl.ds(0, len(NEAR))], near_recv
    ).wait()
    for step in NEAR:
        block = 2 * chip_at(light, step) + depth
        relay(block, columns.at[block])
    share_rims = pltpu.make_async_remote_copy(
        packed.at[depth], packed.at[depth], rim_sem.at[0], rim_sem.at[1],
        device_id=device(light, sibling, height), device_id_type=MESH,
    )
    on_edge = jnp.logical_or(low_edge, high_edge)

    @pl.when(on_edge)
    def _():
        pltpu.make_async_copy(packed.at[0], packed.at[0], rim_recv).wait()
        share_rims.start()

    @pl.loop(BEFORE_RELAY, BEFORE_MARCH)
    def _(m):
        shading(m)

    pltpu.make_async_copy(
        columns.at[pl.ds(0, 2 * len(FAR))], columns.at[pl.ds(0, 2 * len(FAR))], far_recv
    ).wait()
    pltpu.make_async_copy(
        columns.at[pl.ds(0, len(NEAR) + 1)], columns.at[pl.ds(0, len(NEAR) + 1)], relay_sem.at[1]
    ).wait()
    share_lamp.wait_recv()

    def unpacked(rim):
        turned = jnp.where(eighth == 0, pltpu.roll(rim, 96, 1), pltpu.roll(rim, 32, 1))
        return jnp.concatenate([rim, turned], axis=0)

    @pl.when(on_edge)
    def _():
        share_rims.wait_recv()
        pltpu.make_async_copy(lampedge, lampedge, lampedge_sem.at[1]).wait()

        @pl.loop(0, SLABS)
        def _(k):
            for z in range(2):
                edges[2 * k + z] = unpacked(packed[z, k])

    foreign = jnp.logical_or(
        lane < jnp.where(low_edge, 32, 0), lane >= jnp.where(high_edge, 96, 128)
    )
    inside = jnp.logical_and(
        lane >= jnp.where(jnp.logical_and(eighth == 0, height == 0), 32, 0),
        lane < jnp.where(jnp.logical_and(eighth == EIGHTHS - 1, height == heights - 1), 96, 128),
    )
    down = [jnp.full((DEPTH, 128), light_dir[first + i], jnp.int32) == 1 for i in range(2)]
    rate = [extinction[first + i] * -LOG2E for i in range(2)]
    scale = []
    for i in range(2):
        whole = blur_weights[first + i, 0]
        for t in range(1, 25):
            whole = whole + blur_weights[first + i, t]
        scale.append(jnp.where(inside, 1.0 / jnp.full((DEPTH, 128), whole, jnp.float32), 0.0))

    def column_of(k):
        own = columns[pl.ds(2 * k, 2)].reshape(DEPTH, 128)
        return jnp.where(foreign, edges[pl.ds(2 * k, 2)].reshape(DEPTH, 128), own)

    def factors(s):
        ahead, back = column_of(s), column_of(SLABS - 1 - s)
        return tuple(
            jnp.exp2(jnp.where(down[i], back, ahead) * rate[i]) * scale[i] for i in range(2)
        )

    def blurred(plane, i):
        moved = [plane if b == 0 else pltpu.roll(plane, (-b) % 128, 1) for b in range(-2, 3)]
        total = None
        for a in range(-2, 3):
            term = None
            for b in range(5):
                part = (moved[b].reshape(DEPTH // 8, 8, 128) * taps[i, 5 * (a + 2) + b][None]).reshape(DEPTH, 128)
                term = part if term is None else term + part
            if a:
                term = pltpu.roll(term, (-a) % DEPTH, 0)
                term = jnp.where(row >= -a if a < 0 else row < DEPTH - a, term, 0.0)
            total = term if total is None else total + term
        return total

    def advance(s, carry):
        plane, factor = carry
        later = factors(s + 1)
        plane = tuple(blurred(plane[i] * factor[i], i) for i in range(2))
        for i in range(2):
            steps[i, s + 1] = plane[i]
        return plane, later

    start = []
    for i in range(2):
        own = jnp.concatenate([lampbuf[0, i], lampbuf[1, i]], axis=0)
        other = jnp.concatenate([unpacked(lampedge[0, i]), unpacked(lampedge[1, i])], axis=0)
        start.append(jnp.where(foreign, other, own))
        steps[i, 0] = start[i]
    carry = lax.fori_loop(0, SLABS // 2 - 1, advance, (tuple(start), factors(0)))

    def send(k):
        alone = jnp.logical_and(k == light, half == depth)
        to = planes.at[depth * EIGHTHS + eighth]

        @pl.when(alone)
        def _():
            pltpu.make_async_copy(leaving.at[k], to, plane_sem.at[1]).start()

        @pl.when(jnp.logical_not(alone))
        def _():
            pltpu.make_async_remote_copy(
                leaving.at[k], to, plane_sem.at[0], plane_sem.at[1],
                device_id=device(k, half, height), device_id_type=MESH,
            ).start()

    def advance_and_send(j, carry):
        s = j + SLABS // 2 - 1
        carry = advance(s, carry)
        late = carry[0]
        early = [steps[i, SLABS - 2 - s] for i in range(2)]
        front = [jnp.where(down[i], early[i], late[i]) for i in range(2)]
        rear = [jnp.where(down[i], late[i], early[i]) for i in range(2)]
        for k, pair in ((s + 1, front), (SLABS - 2 - s, rear)):
            leaving[k] = jnp.where(lane < 64, pltpu.roll(pair[0], 96, 1), pltpu.roll(pair[1], 32, 1))
            send(k)

        return carry

    lax.fori_loop(0, SLABS // 2, advance_and_send, carry)

    @pl.loop(BEFORE_MARCH, BLOCKS)
    def _(m):
        shading(m)

    pltpu.make_async_copy(planes, planes, plane_sem.at[1]).wait()

    for m in range(BLOCKS):
        lanes = pl.ds(128 * m, 128)
        for pair in range(2):
            even, odd = planes[EIGHTHS * pair + 2 * m], planes[EIGHTHS * pair + 2 * m + 1]
            entering = (
                jnp.where(lane < 64, even, pltpu.roll(odd, 64, 1)),
                jnp.where(lane < 64, pltpu.roll(even, 64, 1), odd),
            )
            for i in range(2):
                c = 2 * pair + i
                seen = jnp.sum(shade[c, m] * entering[i][None], axis=1)
                out[c, :, lanes] = seen * albedo[HALF * depth + c]

    pltpu.make_async_copy(
        columns.at[pl.ds(0, len(NEAR) + 2 * len(FAR))], columns.at[pl.ds(0, len(NEAR) + 2 * len(FAR))], col_send
    ).wait()
    pltpu.make_async_copy(
        columns.at[pl.ds(0, len(NEAR) + 1)], columns.at[pl.ds(0, len(NEAR) + 1)], relay_sem.at[0]
    ).wait()

    @pl.when(has_above)
    def _():
        pltpu.make_async_copy(rims, rims, up_send).wait()

    @pl.when(has_below)
    def _():
        pltpu.make_async_copy(rims, rims, down_send).wait()

    @pl.when(on_edge)
    def _():
        share_rims.wait_send()

    share.wait_send()
    share_lamp.wait_send()

    @pl.when(jnp.logical_or(lamp_up, lamp_down))
    def _():
        pltpu.make_async_copy(lampedge, lampedge, lampedge_sem.at[0]).wait()

    @pl.when(half == depth)
    def _():
        part = leaving.at[pl.ds(0, SLABS - 1)]
        pltpu.make_async_copy(part, part, plane_sem.at[0]).wait()

    @pl.when(half != depth)
    def _():
        pltpu.make_async_copy(leaving, leaving, plane_sem.at[0]).wait()


def local(density, active_list, light_dir, lamp_plane, extinction, blur_weights, albedo):
    f32 = jnp.float32
    vmem = pl.BlockSpec(memory_space=pltpu.VMEM)
    anywhere = pl.BlockSpec(memory_space=pl.ANY)
    dma = pltpu.SemaphoreType.DMA
    return pl.pallas_call(
        body,
        out_shape=jax.ShapeDtypeStruct((HALF, SLICES, WIDTH), f32),
        in_specs=[anywhere] * 7,
        out_specs=vmem,
        scratch_shapes=[
            pltpu.VMEM(active_list.shape, jnp.int32),
            pltpu.SMEM(light_dir.shape, jnp.int32),
            pltpu.SMEM(extinction.shape, f32),
            pltpu.SMEM(blur_weights.shape, f32),
            pltpu.SMEM(albedo.shape, f32),
            pltpu.VMEM((SLICES, ROWS, WIDTH), f32),
            pltpu.VMEM((HALF, ROWS, WIDTH), f32),
            pltpu.VMEM((2, SLICES, ROWS, WIDTH), f32),
            pltpu.VMEM((EIGHTHS, ROWS, 128), f32),
            pltpu.VMEM((2, 8, 128), f32),
            pltpu.VMEM((2 * SLABS, ROWS, 128), f32),
            pltpu.VMEM((2, SLABS, 8, 128), f32),
            pltpu.VMEM((2 * SLABS, ROWS, 128), f32),
            pltpu.VMEM((EIGHTHS, HALF, ROWS, 128), f32),
            pltpu.VMEM((2, HALF, 8, 128), f32),
            pltpu.VMEM((2, 2, ROWS, 128), f32),
            pltpu.VMEM((2, 2, 8, 128), f32),
            pltpu.VMEM((2, SLABS, DEPTH, 128), f32),
            pltpu.VMEM((SLABS, DEPTH, 128), f32),
            pltpu.VMEM((2 * EIGHTHS, DEPTH, 128), f32),
            pltpu.VMEM((HALF, BLOCKS, SLICES, DEPTH, 128), f32),
            pltpu.VMEM((2, 25, 8, 128), f32),
            dma((10,)), dma(()), dma(()), dma(()), dma((2,)), dma(()), dma(()), dma(()), dma((2,)), dma((2,)), dma((2,)), dma((2,)), dma((2,)),
        ],
        compiler_params=pltpu.CompilerParams(
            collective_id=0, has_side_effects=True, vmem_limit_bytes=63 * 1024 * 1024
        ),
        name="march_and_shade",
    )(density, active_list, light_dir, lamp_plane, extinction, blur_weights, albedo)


def solution(mesh):
    in_specs = (
        P("light", "depth", "height"),
        P("depth", None),
        P(),
        P(None, "depth", "height"),
        P(),
        P(),
        P(),
    )
    out_specs = P("depth", "light", "height")
    return jax.shard_map(local, mesh=mesh, in_specs=in_specs, out_specs=out_specs, check_vma=False)
```

```python
import jax
import jax.numpy as jnp
from jax import lax
from jax.experimental import pallas as pl
from jax.experimental.pallas import tpu as pltpu
from jax.sharding import PartitionSpec as P

MESH = pl.DeviceIdType.MESH
LOG2E = 1.4426950408889634
SLICES = 16
SLABS = 16
ROWS = 16
DEPTH = 32
WIDTH = 512
BLOCKS = WIDTH // 128
BRICK_ROWS = 8
EIGHTHS = 8
HALF = 4
BEFORE_RELAY = 1
BEFORE_MARCH = 2
SIDE = 4


def hops(down, right):
    return min(down, SIDE - down) + min(right, SIDE - right)


OTHERS = sorted(
    ((down, right) for down in range(SIDE) for right in range(SIDE) if down or right),
    key=lambda step: -hops(*step),
)
FAR = [step for step in OTHERS if hops(*step) > 2]
NEAR = [step for step in OTHERS if hops(*step) <= 2]


def chip_at(light, step):
    down = lax.rem(lax.div(light, SIDE) + step[0], SIDE)
    return SIDE * down + lax.rem(lax.rem(light, SIDE) + step[1], SIDE)


def half_of(light):
    return 1 - light // EIGHTHS


def eighth_of(light):
    return (light % EIGHTHS // SIDE) * SIDE + (light + 3) % SIDE


def hops_between(one, other):
    total = 0
    for a, b in (
        (one // SIDE, other // SIDE),
        (one % SIDE, other % SIDE),
    ):
        way = lax.rem(a - b + SIDE, SIDE)
        total = total + jnp.minimum(way, SIDE - way)
    return total


def device(light, depth, height):
    return {"light": light, "depth": depth, "height": height}


def windows(block):
    lane = lax.broadcasted_iota(jnp.int32, (block.shape[0], 128), 1)
    parts = [block[:, 128 * m : 128 * m + 128] for m in range(BLOCKS)]
    near = [pltpu.roll(part, 32, 1) for part in parts]
    far = [pltpu.roll(part, 96, 1) for part in parts]
    made = [far[0]]
    for m in range(BLOCKS):
        made.append(near[m] if m == 0 else jnp.where(lane < 32, near[m - 1], near[m]))
        made.append(far[m] if m == BLOCKS - 1 else jnp.where(lane < 96, far[m], far[m + 1]))
    made.append(near[BLOCKS - 1])
    return made


def packed_low(window):
    lane = lax.broadcasted_iota(jnp.int32, (8, 128), 1)
    return jnp.where(lane < 32, window[:8], pltpu.roll(window[8:], 32, 1))


def packed_high(window):
    lane = lax.broadcasted_iota(jnp.int32, (8, 128), 1)
    return jnp.where(lane >= 96, window[:8], pltpu.roll(window[8:], 96, 1))


def spread(rim, turn):
    return jnp.concatenate([rim, pltpu.roll(rim, turn, 1)], axis=0)


def body(
    density, active_hbm, light_dir_hbm, lamp, extinction_hbm, blur_hbm, albedo_hbm,
    out,
    active, light_dir, extinction, blur_weights, albedo, dens, lampv, masked, wins, rims, rims_in, columns, lampwin, lamprim, lampbuf, lampedge, steps, leaving, planes, shade, taps, lifted, image,
    load_sem, col_send, late_send, far_recv, near_recv, relay_sem, up_sem, down_sem, mask_sem, lamp_sem, lampedge_sem, plane_send, plane_recv, out_sem,
):
    light, depth, height = (lax.axis_index(a) for a in ("light", "depth", "height"))
    heights = lax.axis_size("height")
    half, eighth = half_of(light), eighth_of(light)
    sibling = 1 - depth
    has_below, has_above = height > 0, height < heights - 1
    low_edge = jnp.logical_and(eighth == 0, has_below)
    high_edge = jnp.logical_and(eighth == EIGHTHS - 1, has_above)
    mine = 2 * light + depth
    above, below = lax.rem(height + 1, heights), lax.rem(height + heights - 1, heights)
    first = HALF * half + 2 * depth

    chunk = SLICES // 4
    loads = [
        pltpu.make_async_copy(
            density.at[pl.ds(chunk * i, chunk)], dens.at[pl.ds(chunk * i, chunk)], load_sem.at[i]
        )
        for i in range(4)
    ]
    for load in loads:
        load.start()
    barrier = pltpu.get_barrier_semaphore()

    def greet(to, core, at):
        pl.semaphore_signal(barrier, inc=1, device_id=device(to, core, at), device_id_type=MESH)

    for step in FAR:
        for core in range(2):
            greet(chip_at(light, step), core, height)

    @pl.when(has_below)
    def _():
        greet(light, depth, below)

    @pl.when(has_above)
    def _():
        greet(light, depth, above)

    @pl.when(low_edge)
    def _():
        greet(light, sibling, below)

    @pl.when(high_edge)
    def _():
        greet(light, sibling, above)

    for step in NEAR:
        for core in range(2):
            greet(chip_at(light, step), core, height)
    greet(light, sibling, height)

    load_lamp = pltpu.make_async_copy(lamp.at[pl.ds(HALF * half, HALF)], lampv, load_sem.at[4])
    load_lamp.start()
    load_active = pltpu.make_async_copy(active_hbm, active, load_sem.at[5])
    load_small = [
        pltpu.make_async_copy(light_dir_hbm, light_dir, load_sem.at[6]),
        pltpu.make_async_copy(extinction_hbm, extinction, load_sem.at[7]),
        pltpu.make_async_copy(blur_hbm, blur_weights, load_sem.at[8]),
        pltpu.make_async_copy(albedo_hbm, albedo, load_sem.at[9]),
    ]
    load_active.start()
    for load in load_small:
        load.start()

    load_active.wait()
    listed = active[...]
    live = []
    for m in range(BLOCKS):
        brick = light * (BLOCKS * heights) + height * BLOCKS + m
        found = jnp.max(jnp.where(listed == brick, 1.0, 0.0), axis=1, keepdims=True)
        live.append(
            jnp.concatenate(
                [jnp.broadcast_to(found[i : i + 1], (BRICK_ROWS, 128)) for i in range(2)], axis=0
            )
        )
    live = jnp.concatenate(live, axis=1)

    column = jnp.zeros((ROWS, WIDTH), jnp.float32)
    for i in range(4):
        loads[i].wait()
        for x in range(chunk * i, chunk * i + chunk):
            cells = dens[x] * live
            masked[depth, x] = cells
            column = column + cells
    made = windows(column)
    for j in range(EIGHTHS):
        wins[j] = made[j + 1]
    rims[0] = packed_high(made[0])
    rims[1] = packed_low(made[-1])

    lamp_up = jnp.logical_and(eighth == 0, has_above)
    lamp_down = jnp.logical_and(eighth == EIGHTHS - 1, has_below)
    reached = [flag.astype(jnp.int32) for flag in (has_below, has_above, lamp_down, lamp_up)]
    pl.semaphore_wait(barrier, 2 * SLABS - 1 + sum(reached))

    rim_up = pltpu.make_async_remote_copy(
        rims.at[1], rims_in.at[1], up_sem.at[0], up_sem.at[1],
        device_id=device(light, depth, above), device_id_type=MESH,
    )
    rim_down = pltpu.make_async_remote_copy(
        rims.at[0], rims_in.at[0], down_sem.at[0], down_sem.at[1],
        device_id=device(light, depth, below), device_id_type=MESH,
    )

    @pl.when(has_above)
    def _():
        rim_up.start()

    @pl.when(has_below)
    def _():
        rim_down.start()

    def send_window(to, core, arrived, left=col_send):
        pltpu.make_async_remote_copy(
            wins.at[eighth_of(to)], columns.at[mine], left, arrived,
            device_id=device(to, core, height), device_id_type=MESH,
        ).start()

    def at_rim(to):
        return jnp.logical_or(eighth_of(to) == 0, eighth_of(to) == EIGHTHS - 1)

    def send_far(to):
        for core in range(2):
            send_window(to, core, far_recv)

    for step in FAR:
        to = chip_at(light, step)

        @pl.when(jnp.logical_not(at_rim(to)))
        def _():
            send_far(to)

    for step in NEAR:
        to = chip_at(light, step)

        @pl.when(jnp.logical_not(at_rim(to)))
        def _():
            send_window(to, depth, near_recv)

    share = pltpu.make_async_remote_copy(
        masked.at[depth], masked.at[depth], mask_sem.at[0], mask_sem.at[1],
        device_id=device(light, sibling, height), device_id_type=MESH,
    )
    share.start()

    load_lamp.wait()
    for c in range(HALF):
        made = windows(lampv[c])
        for j in range(EIGHTHS):
            lampwin[j, c] = made[j + 1]
        lamprim[0, c] = packed_high(made[0])
        lamprim[1, c] = packed_low(made[-1])
    share_lamp = pltpu.make_async_remote_copy(
        lampwin.at[eighth, pl.ds(2 * sibling, 2)], lampbuf.at[depth], lamp_sem.at[0], lamp_sem.at[1],
        device_id=device(light, sibling, height), device_id_type=MESH,
    )
    share_lamp.start()

    def lamp_over(source, at):
        for to in range(2):
            pltpu.make_async_remote_copy(
                lamprim.at[source, pl.ds(2 * to, 2)], lampedge.at[depth], lampedge_sem.at[0], lampedge_sem.at[1],
                device_id=device(light, to, at), device_id_type=MESH,
            ).start()

    @pl.when(lamp_up)
    def _():
        lamp_over(1, above)

    @pl.when(lamp_down)
    def _():
        lamp_over(0, below)

    lampbuf[depth] = lampwin[eighth, pl.ds(2 * depth, 2)]

    thin = lax.broadcasted_iota(jnp.int32, (ROWS, 128), 1)

    @pl.when(has_below)
    def _():
        rim_up.wait_recv()
        wins[0] = jnp.where(thin < 32, spread(rims_in[1], 96), wins[0])

    @pl.when(has_above)
    def _():
        rim_down.wait_recv()
        wins[EIGHTHS - 1] = jnp.where(thin >= 96, spread(rims_in[0], 32), wins[EIGHTHS - 1])

    ends = [to for to in range(SLABS) if eighth_of(to) in (0, EIGHTHS - 1)]
    for to in ends:
        away = hops_between(to, light)

        @pl.when(away > 2)
        def _():
            send_far(to)

        @pl.when(jnp.logical_and(away > 0, away <= 2))
        def _():
            send_window(to, depth, near_recv)
            send_window(to, sibling, near_recv, late_send.at[ends.index(to)])

    def relay(block, source):
        pltpu.make_async_remote_copy(
            source, columns.at[block], relay_sem.at[0], relay_sem.at[1],
            device_id=device(light, sibling, height), device_id_type=MESH,
        ).start()

    relay(mine, wins.at[eighth])
    columns[mine] = wins[eighth]

    lane = lax.broadcasted_iota(jnp.int32, (DEPTH, 128), 1)
    row = lax.broadcasted_iota(jnp.int32, (DEPTH, 128), 0)

    share.wait_recv()

    for load in load_small:
        load.wait()
    shown = [HALF * depth + i for i in range(HALF)]
    shown_down = [jnp.full((DEPTH, 128), light_dir[c], jnp.int32) == 1 for c in shown]
    shown_rate = [extinction[c] * -LOG2E for c in shown]

    def shading(m):
        lanes = pl.ds(pl.multiple_of(128 * m, 128), 128)

        def cells_of(x):
            return masked[:, x, :, lanes].reshape(DEPTH, 128)

        total = lax.fori_loop(
            0, SLICES, lambda x, t: t + cells_of(x), jnp.zeros((DEPTH, 128), jnp.float32), unroll=True
        )

        def one(x, running):
            cells = cells_of(x)
            after = running + cells
            behind = total - after
            optical = cells * (6.0 / DEPTH)
            summed = optical
            for step in (1, 2, 4, 8, 16):
                summed = summed + jnp.where(row >= step, pltpu.roll(summed, step, 0), 0.0)
            weight = jnp.exp(optical - summed) * (1.0 - jnp.exp(-optical))
            for i in range(HALF):
                before = jnp.where(shown_down[i], behind, running)
                shade[i, m, x] = jnp.exp2(before * shown_rate[i]) * weight
            return after

        def two(i, running):
            return one(2 * i + 1, one(2 * i, running))

        lax.fori_loop(0, SLICES // 2, two, jnp.zeros((DEPTH, 128), jnp.float32))

    for i in range(2):
        for t in range(25):
            taps[i, t] = jnp.full((8, 128), blur_weights[first + i, t], jnp.float32)

    @pl.loop(0, BEFORE_RELAY)
    def _(m):
        shading(m)

    share_lamp.wait_recv()

    on_edge = jnp.logical_or(low_edge, high_edge)

    @pl.when(on_edge)
    def _():
        pltpu.make_async_copy(lampedge, lampedge, lampedge_sem.at[1]).wait()

    def unpacked(rim):
        return jnp.where(jnp.broadcast_to(eighth == 0, (ROWS, 128)), spread(rim, 96), spread(rim, 32))

    foreign = jnp.logical_or(
        lane < jnp.where(low_edge, 32, 0), lane >= jnp.where(high_edge, 96, 128)
    )
    inside = jnp.logical_and(
        lane >= jnp.where(jnp.logical_and(eighth == 0, height == 0), 32, 0),
        lane < jnp.where(jnp.logical_and(eighth == EIGHTHS - 1, height == heights - 1), 96, 128),
    )
    down = [jnp.full((DEPTH, 128), light_dir[first + i], jnp.int32) == 1 for i in range(2)]
    rate = [extinction[first + i] * -LOG2E for i in range(2)]
    scale = []
    for i in range(2):
        whole = blur_weights[first + i, 0]
        for t in range(1, 25):
            whole = whole + blur_weights[first + i, t]
        scale.append(jnp.where(inside, 1.0 / jnp.full((DEPTH, 128), whole, jnp.float32), 0.0))

    for i in range(2):
        lifted[i] = jnp.zeros((DEPTH + 16, 128), jnp.float32)

    start = []
    for i in range(2):
        own = jnp.concatenate([lampbuf[0, i], lampbuf[1, i]], axis=0)
        other = jnp.concatenate([unpacked(lampedge[0, i]), unpacked(lampedge[1, i])], axis=0)
        start.append(jnp.where(foreign, other, own))
        steps[i, 0] = start[i]
    def wait_blocks(count, semaphore):
        some = columns.at[pl.ds(0, count)]
        pltpu.make_async_copy(some, some, semaphore).wait()

    late = at_rim(light)

    @pl.when(jnp.logical_not(late))
    def _():
        wait_blocks(len(NEAR), near_recv)
        for step in NEAR:
            block = 2 * chip_at(light, step) + depth
            relay(block, columns.at[block])

    @pl.loop(BEFORE_RELAY, BEFORE_MARCH)
    def _(m):
        shading(m)

    @pl.when(late)
    def _():
        wait_blocks(2 * len(NEAR), near_recv)
        wait_blocks(1, relay_sem.at[1])

    @pl.when(jnp.logical_not(late))
    def _():
        wait_blocks(len(NEAR) + 1, relay_sem.at[1])

    wait_blocks(2 * len(FAR), far_recv)
    def column_of(k):
        return columns[pl.ds(2 * k, 2)].reshape(DEPTH, 128)

    def factors(s):
        ahead, back = column_of(s), column_of(SLABS - 1 - s)
        return tuple(
            jnp.exp2(jnp.where(down[i], back, ahead) * rate[i]) * scale[i] for i in range(2)
        )

    def blurred(plane, i):
        lifted[i, 8 : 8 + DEPTH] = plane
        moved = [
            plane if a == 0 else lifted[i, 8 + a : 8 + a + DEPTH] for a in range(-2, 3)
        ]
        moved = [part.reshape(DEPTH // 8, 8, 128) for part in moved]
        total = None
        for b in range(-2, 3):
            term = None
            for a in range(5):
                part = moved[a] * taps[i, 5 * a + b + 2][None]
                term = part if term is None else term + part
            term = term.reshape(DEPTH, 128)
            if b:
                term = pltpu.roll(term, (-b) % 128, 1)
            total = term if total is None else total + term
        return total

    def advance(s, carry):
        plane, factor = carry
        later = factors(s + 1)
        plane = tuple(blurred(plane[i] * factor[i], i) for i in range(2))
        for i in range(2):
            steps[i, s + 1] = plane[i]
        return plane, later

    carry = lax.fori_loop(0, SLABS // 2 - 1, advance, (tuple(start), factors(0)))

    own_part = half == depth
    arrived = plane_recv.at[lax.div(eighth, 2)]
    place = planes.at[lax.div(eighth, 2), 2 * lax.rem(eighth, 2) + depth]

    def send(k):
        @pl.when(jnp.logical_not(jnp.logical_and(k == light, own_part)))
        def _():
            pltpu.make_async_remote_copy(
                leaving.at[k], place, plane_send, arrived,
                device_id=device(k, half, height), device_id_type=MESH,
            ).start()

    def advance_and_send(j, carry):
        s = j + SLABS // 2 - 1
        carry = advance(s, carry)
        late = carry[0]
        early = [steps[i, SLABS - 2 - s] for i in range(2)]
        front = [jnp.where(down[i], early[i], late[i]) for i in range(2)]
        rear = [jnp.where(down[i], late[i], early[i]) for i in range(2)]
        for k, pair in ((s + 1, front), (SLABS - 2 - s, rear)):
            leaving[k] = jnp.where(lane < 64, pltpu.roll(pair[0], 96, 1), pltpu.roll(pair[1], 32, 1))
            send(k)

        return carry

    lax.fori_loop(0, SLABS // 2, advance_and_send, carry)

    @pl.when(own_part)
    def _():
        pltpu.make_async_copy(leaving.at[light], place, arrived).start()

    @pl.loop(BEFORE_MARCH, BLOCKS)
    def _(m):
        shading(m)


    copies = []
    for m in range(BLOCKS):
        pltpu.make_async_copy(planes.at[m], planes.at[m], plane_recv.at[m]).wait()
        lanes = pl.ds(128 * m, 128)
        for pair in range(2):
            even, odd = planes[m, pair], planes[m, 2 + pair]
            entering = (
                jnp.where(lane < 64, even, pltpu.roll(odd, 64, 1)),
                jnp.where(lane < 64, pltpu.roll(even, 64, 1), odd),
            )
            for i in range(2):
                c = 2 * pair + i
                seen = jnp.sum(shade[c, m] * entering[i][None], axis=1)
                image[c, :, lanes] = seen * albedo[HALF * depth + c]
        copy = pltpu.make_async_copy(image.at[:, :, lanes], out.at[:, :, lanes], out_sem.at[m])
        copy.start()
        copies.append(copy)

    wait_blocks(len(NEAR) + 2 * len(FAR), col_send)
    for n, to in enumerate(ends):
        away = hops_between(to, light)

        @pl.when(jnp.logical_and(away > 0, away <= 2))
        def _():
            wait_blocks(1, late_send.at[n])

    @pl.when(late)
    def _():
        wait_blocks(1, relay_sem.at[0])

    @pl.when(jnp.logical_not(late))
    def _():
        wait_blocks(len(NEAR) + 1, relay_sem.at[0])

    @pl.when(has_above)
    def _():
        rim_up.wait_send()

    @pl.when(has_below)
    def _():
        rim_down.wait_send()

    share.wait_send()
    share_lamp.wait_send()

    @pl.when(jnp.logical_or(lamp_up, lamp_down))
    def _():
        pltpu.make_async_copy(lampedge, lampedge, lampedge_sem.at[0]).wait()

    @pl.when(own_part)
    def _():
        part = leaving.at[pl.ds(0, SLABS - 1)]
        pltpu.make_async_copy(part, part, plane_send).wait()

    @pl.when(jnp.logical_not(own_part))
    def _():
        pltpu.make_async_copy(leaving, leaving, plane_send).wait()

    for copy in copies:
        copy.wait()


def local(density, active_list, light_dir, lamp_plane, extinction, blur_weights, albedo):
    f32 = jnp.float32
    anywhere = pl.BlockSpec(memory_space=pl.ANY)
    dma = pltpu.SemaphoreType.DMA
    return pl.pallas_call(
        body,
        out_shape=jax.ShapeDtypeStruct((HALF, SLICES, WIDTH), f32),
        in_specs=[anywhere] * 7,
        out_specs=anywhere,
        scratch_shapes=[
            pltpu.VMEM(active_list.shape, jnp.int32),
            pltpu.SMEM(light_dir.shape, jnp.int32),
            pltpu.SMEM(extinction.shape, f32),
            pltpu.SMEM(blur_weights.shape, f32),
            pltpu.SMEM(albedo.shape, f32),
            pltpu.VMEM((SLICES, ROWS, WIDTH), f32),
            pltpu.VMEM((HALF, ROWS, WIDTH), f32),
            pltpu.VMEM((2, SLICES, ROWS, WIDTH), f32),
            pltpu.VMEM((EIGHTHS, ROWS, 128), f32),
            pltpu.VMEM((2, 8, 128), f32),
            pltpu.VMEM((2, 8, 128), f32),
            pltpu.VMEM((2 * SLABS, ROWS, 128), f32),
            pltpu.VMEM((EIGHTHS, HALF, ROWS, 128), f32),
            pltpu.VMEM((2, HALF, 8, 128), f32),
            pltpu.VMEM((2, 2, ROWS, 128), f32),
            pltpu.VMEM((2, 2, 8, 128), f32),
            pltpu.VMEM((2, SLABS, DEPTH, 128), f32),
            pltpu.VMEM((SLABS, DEPTH, 128), f32),
            pltpu.VMEM((BLOCKS, 4, DEPTH, 128), f32),
            pltpu.VMEM((HALF, BLOCKS, SLICES, DEPTH, 128), f32),
            pltpu.VMEM((2, 25, 8, 128), f32),
            pltpu.VMEM((2, DEPTH + 16, 128), f32),
            pltpu.VMEM((HALF, SLICES, WIDTH), f32),
            dma((10,)), dma(()), dma((4,)), dma(()), dma(()), dma((2,)), dma((2,)), dma((2,)), dma((2,)), dma((2,)), dma((2,)),
            dma(()), dma((BLOCKS,)), dma((BLOCKS,)),
        ],
        compiler_params=pltpu.CompilerParams(
            collective_id=0, has_side_effects=True, vmem_limit_bytes=63 * 1024 * 1024
        ),
        name="march_and_shade",
    )(density, active_list, light_dir, lamp_plane, extinction, blur_weights, albedo)


def solution(mesh):
    in_specs = (
        P("light", "depth", "height"),
        P("depth", None),
        P(),
        P(None, "depth", "height"),
        P(),
        P(),
        P(),
    )
    out_specs = P("depth", "light", "height")
    return jax.shard_map(local, mesh=mesh, in_specs=in_specs, out_specs=out_specs, check_vma=False)
```

```python
import jax
import jax.numpy as jnp
from jax import lax
from jax.experimental import pallas as pl
from jax.experimental.pallas import tpu as pltpu
from jax.sharding import PartitionSpec as P

MESH = pl.DeviceIdType.MESH
LOG2E = 1.4426950408889634
SLICES = 16
SLABS = 16
ROWS = 16
DEPTH = 32
WIDTH = 512
BLOCKS = WIDTH // 128
BRICK_ROWS = 8
EIGHTHS = 8
HALF = 4
BEFORE_RELAY = 1
BEFORE_MARCH = 2
SIDE = 4


def hops(down, right):
    return min(down, SIDE - down) + min(right, SIDE - right)


OTHERS = sorted(
    ((down, right) for down in range(SIDE) for right in range(SIDE) if down or right),
    key=lambda step: -hops(*step),
)
FAR = [step for step in OTHERS if hops(*step) > 2]
NEAR = [step for step in OTHERS if hops(*step) <= 2]


def chip_at(light, step):
    down = lax.rem(lax.div(light, SIDE) + step[0], SIDE)
    return SIDE * down + lax.rem(lax.rem(light, SIDE) + step[1], SIDE)


def half_of(light):
    return 1 - light // EIGHTHS


def eighth_of(light):
    return (light % EIGHTHS // SIDE) * SIDE + (light + 3) % SIDE


def hops_between(one, other):
    total = 0
    for a, b in (
        (one // SIDE, other // SIDE),
        (one % SIDE, other % SIDE),
    ):
        way = lax.rem(a - b + SIDE, SIDE)
        total = total + jnp.minimum(way, SIDE - way)
    return total


def device(light, depth, height):
    return {"light": light, "depth": depth, "height": height}


def windows(block):
    lane = lax.broadcasted_iota(jnp.int32, (block.shape[0], 128), 1)
    parts = [block[:, 128 * m : 128 * m + 128] for m in range(BLOCKS)]
    near = [pltpu.roll(part, 32, 1) for part in parts]
    far = [pltpu.roll(part, 96, 1) for part in parts]
    made = [far[0]]
    for m in range(BLOCKS):
        made.append(near[m] if m == 0 else jnp.where(lane < 32, near[m - 1], near[m]))
        made.append(far[m] if m == BLOCKS - 1 else jnp.where(lane < 96, far[m], far[m + 1]))
    made.append(near[BLOCKS - 1])
    return made


def packed_low(window):
    lane = lax.broadcasted_iota(jnp.int32, (8, 128), 1)
    return jnp.where(lane < 32, window[:8], pltpu.roll(window[8:], 32, 1))


def packed_high(window):
    lane = lax.broadcasted_iota(jnp.int32, (8, 128), 1)
    return jnp.where(lane >= 96, window[:8], pltpu.roll(window[8:], 96, 1))


def spread(rim, turn):
    return jnp.concatenate([rim, pltpu.roll(rim, turn, 1)], axis=0)


def body(
    density, active_hbm, light_dir_hbm, lamp, extinction_hbm, blur_hbm, albedo_hbm,
    out,
    active, light_dir, extinction, blur_weights, albedo, dens, lampv, masked, wins, rims, rims_in, columns, lampwin, lamprim, lampbuf, lampedge, steps, leaving, planes, shade, taps, lifted, image,
    load_sem, col_send, late_send, far_recv, near_recv, relay_sem, up_sem, down_sem, mask_sem, lamp_sem, lampedge_sem, plane_send, plane_recv, out_sem,
):
    light, depth, height = (lax.axis_index(a) for a in ("light", "depth", "height"))
    heights = lax.axis_size("height")
    half, eighth = half_of(light), eighth_of(light)
    sibling = 1 - depth
    has_below, has_above = height > 0, height < heights - 1
    low_edge = jnp.logical_and(eighth == 0, has_below)
    high_edge = jnp.logical_and(eighth == EIGHTHS - 1, has_above)
    mine = 2 * light + depth
    above, below = lax.rem(height + 1, heights), lax.rem(height + heights - 1, heights)
    first = HALF * half + 2 * depth

    chunk = SLICES // 4
    loads = [
        pltpu.make_async_copy(
            density.at[pl.ds(chunk * i, chunk)], dens.at[pl.ds(chunk * i, chunk)], load_sem.at[i]
        )
        for i in range(4)
    ]
    load_active = pltpu.make_async_copy(active_hbm, active, load_sem.at[5])
    load_active.start()
    for load in loads:
        load.start()
    barrier = pltpu.get_barrier_semaphore()

    def greet(to, core, at):
        pl.semaphore_signal(barrier, inc=1, device_id=device(to, core, at), device_id_type=MESH)

    for step in FAR:
        for core in range(2):
            greet(chip_at(light, step), core, height)

    @pl.when(has_below)
    def _():
        greet(light, depth, below)

    @pl.when(has_above)
    def _():
        greet(light, depth, above)

    @pl.when(low_edge)
    def _():
        greet(light, sibling, below)

    @pl.when(high_edge)
    def _():
        greet(light, sibling, above)

    for step in NEAR:
        for core in range(2):
            greet(chip_at(light, step), core, height)
    greet(light, sibling, height)

    load_lamp = pltpu.make_async_copy(lamp.at[pl.ds(HALF * half, HALF)], lampv, load_sem.at[4])
    load_lamp.start()
    load_small = [
        pltpu.make_async_copy(light_dir_hbm, light_dir, load_sem.at[6]),
        pltpu.make_async_copy(extinction_hbm, extinction, load_sem.at[7]),
        pltpu.make_async_copy(blur_hbm, blur_weights, load_sem.at[8]),
        pltpu.make_async_copy(albedo_hbm, albedo, load_sem.at[9]),
    ]
    for load in load_small:
        load.start()

    load_active.wait()
    listed = active[...]
    live = []
    for m in range(BLOCKS):
        brick = light * (BLOCKS * heights) + height * BLOCKS + m
        found = jnp.max(jnp.where(listed == brick, 1.0, 0.0), axis=1, keepdims=True)
        live.append(
            jnp.concatenate(
                [jnp.broadcast_to(found[i : i + 1], (BRICK_ROWS, 128)) for i in range(2)], axis=0
            )
        )
    live = jnp.concatenate(live, axis=1)

    column = jnp.zeros((ROWS, WIDTH), jnp.float32)
    for i in range(4):
        loads[i].wait()
        for x in range(chunk * i, chunk * i + chunk):
            cells = dens[x] * live
            masked[depth, x] = cells
            column = column + cells
    made = windows(column)
    for j in range(EIGHTHS):
        wins[j] = made[j + 1]
    rims[0] = packed_high(made[0])
    rims[1] = packed_low(made[-1])

    lamp_up = jnp.logical_and(eighth == 0, has_above)
    lamp_down = jnp.logical_and(eighth == EIGHTHS - 1, has_below)
    reached = [flag.astype(jnp.int32) for flag in (has_below, has_above, lamp_down, lamp_up)]
    pl.semaphore_wait(barrier, 2 * SLABS - 1 + sum(reached))

    rim_up = pltpu.make_async_remote_copy(
        rims.at[1], rims_in.at[1], up_sem.at[0], up_sem.at[1],
        device_id=device(light, depth, above), device_id_type=MESH,
    )
    rim_down = pltpu.make_async_remote_copy(
        rims.at[0], rims_in.at[0], down_sem.at[0], down_sem.at[1],
        device_id=device(light, depth, below), device_id_type=MESH,
    )

    @pl.when(has_above)
    def _():
        rim_up.start()

    @pl.when(has_below)
    def _():
        rim_down.start()

    def send_window(to, core, arrived, left=col_send):
        pltpu.make_async_remote_copy(
            wins.at[eighth_of(to)], columns.at[mine], left, arrived,
            device_id=device(to, core, height), device_id_type=MESH,
        ).start()

    def at_rim(to):
        return jnp.logical_or(eighth_of(to) == 0, eighth_of(to) == EIGHTHS - 1)

    def send_far(to):
        for core in range(2):
            send_window(to, core, far_recv)

    for step in FAR:
        to = chip_at(light, step)

        @pl.when(jnp.logical_not(at_rim(to)))
        def _():
            send_far(to)

    for step in NEAR:
        to = chip_at(light, step)

        @pl.when(jnp.logical_not(at_rim(to)))
        def _():
            send_window(to, depth, near_recv)

    share = pltpu.make_async_remote_copy(
        masked.at[depth], masked.at[depth], mask_sem.at[0], mask_sem.at[1],
        device_id=device(light, sibling, height), device_id_type=MESH,
    )
    share.start()

    load_lamp.wait()
    for c in range(HALF):
        made = windows(lampv[c])
        for j in range(EIGHTHS):
            lampwin[j, c] = made[j + 1]
        lamprim[0, c] = packed_high(made[0])
        lamprim[1, c] = packed_low(made[-1])
    share_lamp = pltpu.make_async_remote_copy(
        lampwin.at[eighth, pl.ds(2 * sibling, 2)], lampbuf.at[depth], lamp_sem.at[0], lamp_sem.at[1],
        device_id=device(light, sibling, height), device_id_type=MESH,
    )
    share_lamp.start()

    def lamp_over(source, at):
        for to in range(2):
            pltpu.make_async_remote_copy(
                lamprim.at[source, pl.ds(2 * to, 2)], lampedge.at[depth], lampedge_sem.at[0], lampedge_sem.at[1],
                device_id=device(light, to, at), device_id_type=MESH,
            ).start()

    @pl.when(lamp_up)
    def _():
        lamp_over(1, above)

    @pl.when(lamp_down)
    def _():
        lamp_over(0, below)

    lampbuf[depth] = lampwin[eighth, pl.ds(2 * depth, 2)]

    thin = lax.broadcasted_iota(jnp.int32, (ROWS, 128), 1)

    @pl.when(has_below)
    def _():
        rim_up.wait_recv()
        wins[0] = jnp.where(thin < 32, spread(rims_in[1], 96), wins[0])

    @pl.when(has_above)
    def _():
        rim_down.wait_recv()
        wins[EIGHTHS - 1] = jnp.where(thin >= 96, spread(rims_in[0], 32), wins[EIGHTHS - 1])

    ends = [to for to in range(SLABS) if eighth_of(to) in (0, EIGHTHS - 1)]
    for to in ends:

        @pl.when(hops_between(to, light) > 2)
        def _():
            send_far(to)

    for to in ends:
        away = hops_between(to, light)

        @pl.when(jnp.logical_and(away > 0, away <= 2))
        def _():
            send_window(to, depth, near_recv)
            send_window(to, sibling, near_recv, late_send.at[ends.index(to)])

    def relay(block, source):
        pltpu.make_async_remote_copy(
            source, columns.at[block], relay_sem.at[0], relay_sem.at[1],
            device_id=device(light, sibling, height), device_id_type=MESH,
        ).start()

    relay(mine, wins.at[eighth])
    columns[mine] = wins[eighth]

    lane = lax.broadcasted_iota(jnp.int32, (DEPTH, 128), 1)
    row = lax.broadcasted_iota(jnp.int32, (DEPTH, 128), 0)

    share.wait_recv()

    for load in load_small:
        load.wait()
    shown = [HALF * depth + i for i in range(HALF)]
    shown_down = [jnp.full((DEPTH, 128), light_dir[c], jnp.int32) == 1 for c in shown]
    shown_rate = [extinction[c] * -LOG2E for c in shown]

    def shading(m):
        lanes = pl.ds(pl.multiple_of(128 * m, 128), 128)

        def cells_of(x):
            return masked[:, x, :, lanes].reshape(DEPTH, 128)

        total = lax.fori_loop(
            0, SLICES, lambda x, t: t + cells_of(x), jnp.zeros((DEPTH, 128), jnp.float32), unroll=True
        )

        def one(x, running):
            cells = cells_of(x)
            after = running + cells
            behind = total - after
            optical = cells * (6.0 / DEPTH)
            summed = optical
            for step in (1, 2, 4, 8, 16):
                summed = summed + jnp.where(row >= step, pltpu.roll(summed, step, 0), 0.0)
            weight = jnp.exp(optical - summed) * (1.0 - jnp.exp(-optical))
            for i in range(HALF):
                before = jnp.where(shown_down[i], behind, running)
                shade[i, m, x] = jnp.exp2(before * shown_rate[i]) * weight
            return after

        def two(i, running):
            return one(2 * i + 1, one(2 * i, running))

        lax.fori_loop(0, SLICES // 2, two, jnp.zeros((DEPTH, 128), jnp.float32))

    for i in range(2):
        for t in range(25):
            taps[i, t] = jnp.full((8, 128), blur_weights[first + i, t], jnp.float32)

    @pl.loop(0, BEFORE_RELAY)
    def _(m):
        shading(m)

    share_lamp.wait_recv()

    on_edge = jnp.logical_or(low_edge, high_edge)

    @pl.when(on_edge)
    def _():
        pltpu.make_async_copy(lampedge, lampedge, lampedge_sem.at[1]).wait()

    def unpacked(rim):
        return jnp.where(jnp.broadcast_to(eighth == 0, (ROWS, 128)), spread(rim, 96), spread(rim, 32))

    foreign = jnp.logical_or(
        lane < jnp.where(low_edge, 32, 0), lane >= jnp.where(high_edge, 96, 128)
    )
    inside = jnp.logical_and(
        lane >= jnp.where(jnp.logical_and(eighth == 0, height == 0), 32, 0),
        lane < jnp.where(jnp.logical_and(eighth == EIGHTHS - 1, height == heights - 1), 96, 128),
    )
    down = [jnp.full((DEPTH, 128), light_dir[first + i], jnp.int32) == 1 for i in range(2)]
    rate = [extinction[first + i] * -LOG2E for i in range(2)]
    scale = []
    for i in range(2):
        whole = blur_weights[first + i, 0]
        for t in range(1, 25):
            whole = whole + blur_weights[first + i, t]
        scale.append(jnp.where(inside, 1.0 / jnp.full((DEPTH, 128), whole, jnp.float32), 0.0))

    for i in range(2):
        lifted[i] = jnp.zeros((DEPTH + 16, 128), jnp.float32)

    start = []
    for i in range(2):
        own = jnp.concatenate([lampbuf[0, i], lampbuf[1, i]], axis=0)
        other = jnp.concatenate([unpacked(lampedge[0, i]), unpacked(lampedge[1, i])], axis=0)
        start.append(jnp.where(foreign, other, own))
        steps[i, 0] = start[i]
    def wait_blocks(count, semaphore):
        some = columns.at[pl.ds(0, count)]
        pltpu.make_async_copy(some, some, semaphore).wait()

    late = at_rim(light)

    @pl.when(jnp.logical_not(late))
    def _():
        wait_blocks(len(NEAR), near_recv)
        for step in NEAR:
            block = 2 * chip_at(light, step) + depth
            relay(block, columns.at[block])

    @pl.loop(BEFORE_RELAY, BEFORE_MARCH)
    def _(m):
        shading(m)

    @pl.when(late)
    def _():
        wait_blocks(2 * len(NEAR), near_recv)
        wait_blocks(1, relay_sem.at[1])

    @pl.when(jnp.logical_not(late))
    def _():
        wait_blocks(len(NEAR) + 1, relay_sem.at[1])

    wait_blocks(2 * len(FAR), far_recv)
    def column_of(k):
        return columns[pl.ds(2 * k, 2)].reshape(DEPTH, 128)

    def factors(s):
        ahead, back = column_of(s), column_of(SLABS - 1 - s)
        return tuple(
            jnp.exp2(jnp.where(down[i], back, ahead) * rate[i]) * scale[i] for i in range(2)
        )

    def blurred(plane, i):
        lifted[i, 8 : 8 + DEPTH] = plane
        moved = [
            plane if a == 0 else lifted[i, 8 + a : 8 + a + DEPTH] for a in range(-2, 3)
        ]
        moved = [part.reshape(DEPTH // 8, 8, 128) for part in moved]
        total = None
        for b in range(-2, 3):
            term = None
            for a in range(5):
                part = moved[a] * taps[i, 5 * a + b + 2][None]
                term = part if term is None else term + part
            term = term.reshape(DEPTH, 128)
            if b:
                term = pltpu.roll(term, (-b) % 128, 1)
            total = term if total is None else total + term
        return total

    def advance(s, carry):
        plane, factor = carry
        later = factors(s + 1)
        plane = tuple(blurred(plane[i] * factor[i], i) for i in range(2))
        for i in range(2):
            steps[i, s + 1] = plane[i]
        return plane, later

    carry = lax.fori_loop(0, SLABS // 2 - 1, advance, (tuple(start), factors(0)))

    own_part = half == depth
    arrived = plane_recv.at[lax.div(eighth, 2)]
    place = planes.at[lax.div(eighth, 2), 2 * lax.rem(eighth, 2) + depth]

    def send(k):
        @pl.when(jnp.logical_not(jnp.logical_and(k == light, own_part)))
        def _():
            pltpu.make_async_remote_copy(
                leaving.at[k], place, plane_send, arrived,
                device_id=device(k, half, height), device_id_type=MESH,
            ).start()

    def advance_and_send(j, carry):
        s = j + SLABS // 2 - 1
        carry = advance(s, carry)
        late = carry[0]
        early = [steps[i, SLABS - 2 - s] for i in range(2)]
        front = [jnp.where(down[i], early[i], late[i]) for i in range(2)]
        rear = [jnp.where(down[i], late[i], early[i]) for i in range(2)]
        for k, pair in ((s + 1, front), (SLABS - 2 - s, rear)):
            leaving[k] = jnp.where(lane < 64, pltpu.roll(pair[0], 96, 1), pltpu.roll(pair[1], 32, 1))
            send(k)

        return carry

    lax.fori_loop(0, SLABS // 2, advance_and_send, carry)

    @pl.when(own_part)
    def _():
        pltpu.make_async_copy(leaving.at[light], place, arrived).start()

    @pl.loop(BEFORE_MARCH, BLOCKS)
    def _(m):
        shading(m)


    copies = []
    for m in (1, 2, 3, 0):
        pltpu.make_async_copy(planes.at[m], planes.at[m], plane_recv.at[m]).wait()
        lanes = pl.ds(128 * m, 128)
        for pair in range(2):
            even, odd = planes[m, pair], planes[m, 2 + pair]
            entering = (
                jnp.where(lane < 64, even, pltpu.roll(odd, 64, 1)),
                jnp.where(lane < 64, pltpu.roll(even, 64, 1), odd),
            )
            for i in range(2):
                c = 2 * pair + i
                seen = jnp.sum(shade[c, m] * entering[i][None], axis=1)
                image[c, :, lanes] = seen * albedo[HALF * depth + c]
        copy = pltpu.make_async_copy(image.at[:, :, lanes], out.at[:, :, lanes], out_sem.at[m])
        copy.start()
        copies.append(copy)

    wait_blocks(len(NEAR) + 2 * len(FAR), col_send)
    for n, to in enumerate(ends):
        away = hops_between(to, light)

        @pl.when(jnp.logical_and(away > 0, away <= 2))
        def _():
            wait_blocks(1, late_send.at[n])

    @pl.when(late)
    def _():
        wait_blocks(1, relay_sem.at[0])

    @pl.when(jnp.logical_not(late))
    def _():
        wait_blocks(len(NEAR) + 1, relay_sem.at[0])

    @pl.when(has_above)
    def _():
        rim_up.wait_send()

    @pl.when(has_below)
    def _():
        rim_down.wait_send()

    share.wait_send()
    share_lamp.wait_send()

    @pl.when(jnp.logical_or(lamp_up, lamp_down))
    def _():
        pltpu.make_async_copy(lampedge, lampedge, lampedge_sem.at[0]).wait()

    @pl.when(own_part)
    def _():
        part = leaving.at[pl.ds(0, SLABS - 1)]
        pltpu.make_async_copy(part, part, plane_send).wait()

    @pl.when(jnp.logical_not(own_part))
    def _():
        pltpu.make_async_copy(leaving, leaving, plane_send).wait()

    for copy in copies:
        copy.wait()


def local(density, active_list, light_dir, lamp_plane, extinction, blur_weights, albedo):
    f32 = jnp.float32
    anywhere = pl.BlockSpec(memory_space=pl.ANY)
    dma = pltpu.SemaphoreType.DMA
    return pl.pallas_call(
        body,
        out_shape=jax.ShapeDtypeStruct((HALF, SLICES, WIDTH), f32),
        in_specs=[anywhere] * 7,
        out_specs=anywhere,
        scratch_shapes=[
            pltpu.VMEM(active_list.shape, jnp.int32),
            pltpu.SMEM(light_dir.shape, jnp.int32),
            pltpu.SMEM(extinction.shape, f32),
            pltpu.SMEM(blur_weights.shape, f32),
            pltpu.SMEM(albedo.shape, f32),
            pltpu.VMEM((SLICES, ROWS, WIDTH), f32),
            pltpu.VMEM((HALF, ROWS, WIDTH), f32),
            pltpu.VMEM((2, SLICES, ROWS, WIDTH), f32),
            pltpu.VMEM((EIGHTHS, ROWS, 128), f32),
            pltpu.VMEM((2, 8, 128), f32),
            pltpu.VMEM((2, 8, 128), f32),
            pltpu.VMEM((2 * SLABS, ROWS, 128), f32),
            pltpu.VMEM((EIGHTHS, HALF, ROWS, 128), f32),
            pltpu.VMEM((2, HALF, 8, 128), f32),
            pltpu.VMEM((2, 2, ROWS, 128), f32),
            pltpu.VMEM((2, 2, 8, 128), f32),
            pltpu.VMEM((2, SLABS, DEPTH, 128), f32),
            pltpu.VMEM((SLABS, DEPTH, 128), f32),
            pltpu.VMEM((BLOCKS, 4, DEPTH, 128), f32),
            pltpu.VMEM((HALF, BLOCKS, SLICES, DEPTH, 128), f32),
            pltpu.VMEM((2, 25, 8, 128), f32),
            pltpu.VMEM((2, DEPTH + 16, 128), f32),
            pltpu.VMEM((HALF, SLICES, WIDTH), f32),
            dma((10,)), dma(()), dma((4,)), dma(()), dma(()), dma((2,)), dma((2,)), dma((2,)), dma((2,)), dma((2,)), dma((2,)),
            dma(()), dma((BLOCKS,)), dma((BLOCKS,)),
        ],
        compiler_params=pltpu.CompilerParams(
            collective_id=0, has_side_effects=True, vmem_limit_bytes=63 * 1024 * 1024
        ),
        name="march_and_shade",
    )(density, active_list, light_dir, lamp_plane, extinction, blur_weights, albedo)


def solution(mesh):
    in_specs = (
        P("light", "depth", "height"),
        P("depth", None),
        P(),
        P(None, "depth", "height"),
        P(),
        P(),
        P(),
    )
    out_specs = P("depth", "light", "height")
    return jax.shard_map(local, mesh=mesh, in_specs=in_specs, out_specs=out_specs, check_vma=False)
```

```python
import jax
import jax.numpy as jnp
from jax import lax
from jax.experimental import pallas as pl
from jax.experimental.pallas import tpu as pltpu
from jax.sharding import PartitionSpec as P

MESH = pl.DeviceIdType.MESH
LOG2E = 1.4426950408889634
SLICES = 16
SLABS = 16
ROWS = 16
DEPTH = 32
WIDTH = 512
BLOCKS = WIDTH // 128
BRICK_ROWS = 8
EIGHTHS = 8
HALF = 4
BEFORE_RELAY = 0
BEFORE_MARCH = 1
SIDE = 4


def hops(down, right):
    return min(down, SIDE - down) + min(right, SIDE - right)


OTHERS = sorted(
    ((down, right) for down in range(SIDE) for right in range(SIDE) if down or right),
    key=lambda step: -hops(*step),
)
FAR = [step for step in OTHERS if hops(*step) > 2]
NEAR = [step for step in OTHERS if hops(*step) <= 2]


def chip_at(light, step):
    down = lax.rem(lax.div(light, SIDE) + step[0], SIDE)
    return SIDE * down + lax.rem(lax.rem(light, SIDE) + step[1], SIDE)


def half_of(light):
    return 1 - light // EIGHTHS


def eighth_of(light):
    return (light % EIGHTHS // SIDE) * SIDE + (light + 3) % SIDE


def hops_between(one, other):
    total = 0
    for a, b in (
        (one // SIDE, other // SIDE),
        (one % SIDE, other % SIDE),
    ):
        way = lax.rem(a - b + SIDE, SIDE)
        total = total + jnp.minimum(way, SIDE - way)
    return total


def device(light, depth, height):
    return {"light": light, "depth": depth, "height": height}


def windows(block):
    lane = lax.broadcasted_iota(jnp.int32, (block.shape[0], 128), 1)
    parts = [block[:, 128 * m : 128 * m + 128] for m in range(BLOCKS)]
    near = [pltpu.roll(part, 32, 1) for part in parts]
    far = [pltpu.roll(part, 96, 1) for part in parts]
    made = [far[0]]
    for m in range(BLOCKS):
        made.append(near[m] if m == 0 else jnp.where(lane < 32, near[m - 1], near[m]))
        made.append(far[m] if m == BLOCKS - 1 else jnp.where(lane < 96, far[m], far[m + 1]))
    made.append(near[BLOCKS - 1])
    return made


def packed_low(window):
    lane = lax.broadcasted_iota(jnp.int32, (8, 128), 1)
    return jnp.where(lane < 32, window[:8], pltpu.roll(window[8:], 32, 1))


def packed_high(window):
    lane = lax.broadcasted_iota(jnp.int32, (8, 128), 1)
    return jnp.where(lane >= 96, window[:8], pltpu.roll(window[8:], 96, 1))


def spread(rim, turn):
    return jnp.concatenate([rim, pltpu.roll(rim, turn, 1)], axis=0)


def body(
    density, active_hbm, light_dir_hbm, lamp, extinction_hbm, blur_hbm, albedo_hbm,
    out,
    active, light_dir, extinction, blur_weights, albedo, dens, lampv, masked, wins, rims, rims_in, columns, lampwin, lamprim, lampbuf, lampedge, steps, leaving, planes, shade, taps, lifted, image,
    load_sem, col_send, late_send, far_recv, near_recv, relay_sem, up_sem, down_sem, mask_sem, lamp_sem, lampedge_sem, plane_send, plane_recv, out_sem,
):
    light, depth, height = (lax.axis_index(a) for a in ("light", "depth", "height"))
    heights = lax.axis_size("height")
    half, eighth = half_of(light), eighth_of(light)
    sibling = 1 - depth
    has_below, has_above = height > 0, height < heights - 1
    low_edge = jnp.logical_and(eighth == 0, has_below)
    high_edge = jnp.logical_and(eighth == EIGHTHS - 1, has_above)
    mine = 2 * light + depth
    above, below = lax.rem(height + 1, heights), lax.rem(height + heights - 1, heights)
    first = HALF * half + 2 * depth

    chunk = SLICES // 4
    loads = [
        pltpu.make_async_copy(
            density.at[pl.ds(chunk * i, chunk)], dens.at[pl.ds(chunk * i, chunk)], load_sem.at[i]
        )
        for i in range(4)
    ]
    load_active = pltpu.make_async_copy(active_hbm, active, load_sem.at[5])
    load_active.start()
    for load in loads:
        load.start()
    barrier = pltpu.get_barrier_semaphore()

    def greet(to, core, at):
        pl.semaphore_signal(barrier, inc=1, device_id=device(to, core, at), device_id_type=MESH)

    @pl.when(has_below)
    def _():
        greet(light, depth, below)

    @pl.when(has_above)
    def _():
        greet(light, depth, above)

    @pl.when(low_edge)
    def _():
        greet(light, sibling, below)

    @pl.when(high_edge)
    def _():
        greet(light, sibling, above)

    for step in FAR:
        for core in range(2):
            greet(chip_at(light, step), core, height)

    for step in NEAR:
        for core in range(2):
            greet(chip_at(light, step), core, height)
    greet(light, sibling, height)

    load_lamp = pltpu.make_async_copy(lamp.at[pl.ds(HALF * half, HALF)], lampv, load_sem.at[4])
    load_lamp.start()
    load_small = [
        pltpu.make_async_copy(light_dir_hbm, light_dir, load_sem.at[6]),
        pltpu.make_async_copy(extinction_hbm, extinction, load_sem.at[7]),
        pltpu.make_async_copy(blur_hbm, blur_weights, load_sem.at[8]),
        pltpu.make_async_copy(albedo_hbm, albedo, load_sem.at[9]),
    ]
    for load in load_small:
        load.start()

    load_active.wait()
    listed = active[...]
    live = []
    for m in range(BLOCKS):
        brick = light * (BLOCKS * heights) + height * BLOCKS + m
        found = jnp.max(jnp.where(listed == brick, 1.0, 0.0), axis=1, keepdims=True)
        live.append(
            jnp.concatenate(
                [jnp.broadcast_to(found[i : i + 1], (BRICK_ROWS, 128)) for i in range(2)], axis=0
            )
        )
    live = jnp.concatenate(live, axis=1)

    column = jnp.zeros((ROWS, WIDTH), jnp.float32)
    for i in range(4):
        loads[i].wait()
        for x in range(chunk * i, chunk * i + chunk):
            cells = dens[x] * live
            masked[depth, x] = cells
            column = column + cells
    made = windows(column)
    for j in range(EIGHTHS):
        wins[j] = made[j + 1]
    rims[0] = packed_high(made[0])
    rims[1] = packed_low(made[-1])

    lamp_up = jnp.logical_and(eighth == 0, has_above)
    lamp_down = jnp.logical_and(eighth == EIGHTHS - 1, has_below)
    reached = [flag.astype(jnp.int32) for flag in (has_below, has_above, lamp_down, lamp_up)]
    pl.semaphore_wait(barrier, 2 * SLABS - 1 + sum(reached))

    rim_up = pltpu.make_async_remote_copy(
        rims.at[1], rims_in.at[1], up_sem.at[0], up_sem.at[1],
        device_id=device(light, depth, above), device_id_type=MESH,
    )
    rim_down = pltpu.make_async_remote_copy(
        rims.at[0], rims_in.at[0], down_sem.at[0], down_sem.at[1],
        device_id=device(light, depth, below), device_id_type=MESH,
    )

    @pl.when(has_above)
    def _():
        rim_up.start()

    @pl.when(has_below)
    def _():
        rim_down.start()

    def send_window(to, core, arrived, left=col_send):
        pltpu.make_async_remote_copy(
            wins.at[eighth_of(to)], columns.at[mine], left, arrived,
            device_id=device(to, core, height), device_id_type=MESH,
        ).start()

    def at_rim(to):
        return jnp.logical_or(eighth_of(to) == 0, eighth_of(to) == EIGHTHS - 1)

    def send_far(to):
        for core in range(2):
            send_window(to, core, far_recv)

    for step in FAR:
        to = chip_at(light, step)

        @pl.when(jnp.logical_not(at_rim(to)))
        def _():
            send_far(to)

    for step in NEAR:
        to = chip_at(light, step)

        @pl.when(jnp.logical_not(at_rim(to)))
        def _():
            send_window(to, depth, near_recv)

    share = pltpu.make_async_remote_copy(
        masked.at[depth], masked.at[depth], mask_sem.at[0], mask_sem.at[1],
        device_id=device(light, sibling, height), device_id_type=MESH,
    )
    share.start()

    load_lamp.wait()
    for c in range(HALF):
        made = windows(lampv[c])
        for j in range(EIGHTHS):
            lampwin[j, c] = made[j + 1]
        lamprim[0, c] = packed_high(made[0])
        lamprim[1, c] = packed_low(made[-1])
    share_lamp = pltpu.make_async_remote_copy(
        lampwin.at[eighth, pl.ds(2 * sibling, 2)], lampbuf.at[depth], lamp_sem.at[0], lamp_sem.at[1],
        device_id=device(light, sibling, height), device_id_type=MESH,
    )
    share_lamp.start()

    def lamp_over(source, at):
        for to in range(2):
            pltpu.make_async_remote_copy(
                lamprim.at[source, pl.ds(2 * to, 2)], lampedge.at[depth], lampedge_sem.at[0], lampedge_sem.at[1],
                device_id=device(light, to, at), device_id_type=MESH,
            ).start()

    @pl.when(lamp_up)
    def _():
        lamp_over(1, above)

    @pl.when(lamp_down)
    def _():
        lamp_over(0, below)

    lampbuf[depth] = lampwin[eighth, pl.ds(2 * depth, 2)]

    thin = lax.broadcasted_iota(jnp.int32, (ROWS, 128), 1)

    @pl.when(has_below)
    def _():
        rim_up.wait_recv()
        wins[0] = jnp.where(thin < 32, spread(rims_in[1], 96), wins[0])

    @pl.when(has_above)
    def _():
        rim_down.wait_recv()
        wins[EIGHTHS - 1] = jnp.where(thin >= 96, spread(rims_in[0], 32), wins[EIGHTHS - 1])

    ends = [to for to in range(SLABS) if eighth_of(to) in (0, EIGHTHS - 1)]
    for to in ends:

        @pl.when(hops_between(to, light) > 2)
        def _():
            send_far(to)

    for to in ends:
        away = hops_between(to, light)

        @pl.when(jnp.logical_and(away > 0, away <= 2))
        def _():
            send_window(to, depth, near_recv)
            send_window(to, sibling, near_recv, late_send.at[ends.index(to)])

    def relay(block, source):
        pltpu.make_async_remote_copy(
            source, columns.at[block], relay_sem.at[0], relay_sem.at[1],
            device_id=device(light, sibling, height), device_id_type=MESH,
        ).start()

    relay(mine, wins.at[eighth])
    columns[mine] = wins[eighth]

    lane = lax.broadcasted_iota(jnp.int32, (DEPTH, 128), 1)
    row = lax.broadcasted_iota(jnp.int32, (DEPTH, 128), 0)

    share.wait_recv()

    for load in load_small:
        load.wait()
    shown = [HALF * depth + i for i in range(HALF)]
    shown_down = [jnp.full((DEPTH, 128), light_dir[c], jnp.int32) == 1 for c in shown]
    shown_rate = [extinction[c] * -LOG2E for c in shown]

    def shading(m):
        lanes = pl.ds(pl.multiple_of(128 * m, 128), 128)

        def cells_of(x):
            return masked[:, x, :, lanes].reshape(DEPTH, 128)

        total = lax.fori_loop(
            0, SLICES, lambda x, t: t + cells_of(x), jnp.zeros((DEPTH, 128), jnp.float32), unroll=True
        )

        def one(x, running):
            cells = cells_of(x)
            after = running + cells
            behind = total - after
            optical = cells * (6.0 / DEPTH)
            summed = optical
            for step in (1, 2, 4, 8, 16):
                summed = summed + jnp.where(row >= step, pltpu.roll(summed, step, 0), 0.0)
            weight = jnp.exp(optical - summed) * (1.0 - jnp.exp(-optical))
            for i in range(HALF):
                before = jnp.where(shown_down[i], behind, running)
                shade[i, m, x] = jnp.exp2(before * shown_rate[i]) * weight
            return after

        def two(i, running):
            return one(2 * i + 1, one(2 * i, running))

        lax.fori_loop(0, SLICES // 2, two, jnp.zeros((DEPTH, 128), jnp.float32))

    for i in range(2):
        for t in range(25):
            taps[i, t] = jnp.full((8, 128), blur_weights[first + i, t], jnp.float32)

    @pl.loop(0, BEFORE_RELAY)
    def _(m):
        shading(m)

    share_lamp.wait_recv()

    on_edge = jnp.logical_or(low_edge, high_edge)

    @pl.when(on_edge)
    def _():
        pltpu.make_async_copy(lampedge, lampedge, lampedge_sem.at[1]).wait()

    def unpacked(rim):
        return jnp.where(jnp.broadcast_to(eighth == 0, (ROWS, 128)), spread(rim, 96), spread(rim, 32))

    foreign = jnp.logical_or(
        lane < jnp.where(low_edge, 32, 0), lane >= jnp.where(high_edge, 96, 128)
    )
    inside = jnp.logical_and(
        lane >= jnp.where(jnp.logical_and(eighth == 0, height == 0), 32, 0),
        lane < jnp.where(jnp.logical_and(eighth == EIGHTHS - 1, height == heights - 1), 96, 128),
    )
    down = [jnp.full((DEPTH, 128), light_dir[first + i], jnp.int32) == 1 for i in range(2)]
    rate = [extinction[first + i] * -LOG2E for i in range(2)]
    scale = []
    for i in range(2):
        whole = blur_weights[first + i, 0]
        for t in range(1, 25):
            whole = whole + blur_weights[first + i, t]
        scale.append(jnp.where(inside, 1.0 / jnp.full((DEPTH, 128), whole, jnp.float32), 0.0))

    for i in range(2):
        lifted[i] = jnp.zeros((DEPTH + 16, 128), jnp.float32)

    start = []
    for i in range(2):
        own = jnp.concatenate([lampbuf[0, i], lampbuf[1, i]], axis=0)
        other = jnp.concatenate([unpacked(lampedge[0, i]), unpacked(lampedge[1, i])], axis=0)
        start.append(jnp.where(foreign, other, own))
        steps[i, 0] = start[i]
    def wait_blocks(count, semaphore):
        some = columns.at[pl.ds(0, count)]
        pltpu.make_async_copy(some, some, semaphore).wait()

    late = at_rim(light)

    @pl.when(jnp.logical_not(late))
    def _():
        wait_blocks(len(NEAR), near_recv)
        for step in NEAR:
            block = 2 * chip_at(light, step) + depth
            relay(block, columns.at[block])

    @pl.loop(BEFORE_RELAY, BEFORE_MARCH)
    def _(m):
        shading(m)

    @pl.when(late)
    def _():
        wait_blocks(2 * len(NEAR), near_recv)
        wait_blocks(1, relay_sem.at[1])

    @pl.when(jnp.logical_not(late))
    def _():
        wait_blocks(len(NEAR) + 1, relay_sem.at[1])

    wait_blocks(2 * len(FAR), far_recv)
    def column_of(k):
        return columns[pl.ds(2 * k, 2)].reshape(DEPTH, 128)

    def factors(s):
        ahead, back = column_of(s), column_of(SLABS - 1 - s)
        return tuple(
            jnp.exp2(jnp.where(down[i], back, ahead) * rate[i]) * scale[i] for i in range(2)
        )

    def blurred(plane, i):
        lifted[i, 8 : 8 + DEPTH] = plane
        moved = [
            plane if a == 0 else lifted[i, 8 + a : 8 + a + DEPTH] for a in range(-2, 3)
        ]
        moved = [part.reshape(DEPTH // 8, 8, 128) for part in moved]
        total = None
        for b in range(-2, 3):
            term = None
            for a in range(5):
                part = moved[a] * taps[i, 5 * a + b + 2][None]
                term = part if term is None else term + part
            term = term.reshape(DEPTH, 128)
            if b:
                term = pltpu.roll(term, (-b) % 128, 1)
            total = term if total is None else total + term
        return total

    def advance(s, carry):
        plane, factor = carry
        later = factors(s + 1)
        plane = tuple(blurred(plane[i] * factor[i], i) for i in range(2))
        for i in range(2):
            steps[i, s + 1] = plane[i]
        return plane, later

    carry = lax.fori_loop(0, SLABS // 2 - 1, advance, (tuple(start), factors(0)), unroll=True)

    own_part = half == depth
    arrived = plane_recv.at[lax.div(eighth, 2)]
    place = planes.at[lax.div(eighth, 2), 2 * lax.rem(eighth, 2) + depth]

    def send(k):
        @pl.when(jnp.logical_not(jnp.logical_and(k == light, own_part)))
        def _():
            pltpu.make_async_remote_copy(
                leaving.at[k], place, plane_send, arrived,
                device_id=device(k, half, height), device_id_type=MESH,
            ).start()

    def advance_and_send(j, carry):
        s = j + SLABS // 2 - 1
        carry = advance(s, carry)
        late = carry[0]
        early = [steps[i, SLABS - 2 - s] for i in range(2)]
        front = [jnp.where(down[i], early[i], late[i]) for i in range(2)]
        rear = [jnp.where(down[i], late[i], early[i]) for i in range(2)]
        for k, pair in ((s + 1, front), (SLABS - 2 - s, rear)):
            leaving[k] = jnp.where(lane < 64, pltpu.roll(pair[0], 96, 1), pltpu.roll(pair[1], 32, 1))
            send(k)

        return carry

    lax.fori_loop(0, SLABS // 2, advance_and_send, carry, unroll=True)

    @pl.when(own_part)
    def _():
        pltpu.make_async_copy(leaving.at[light], place, arrived).start()

    @pl.loop(BEFORE_MARCH, BLOCKS)
    def _(m):
        shading(m)


    copies = []
    for m in (1, 2, 3, 0):
        pltpu.make_async_copy(planes.at[m], planes.at[m], plane_recv.at[m]).wait()
        lanes = pl.ds(128 * m, 128)
        for pair in range(2):
            even, odd = planes[m, pair], planes[m, 2 + pair]
            entering = (
                jnp.where(lane < 64, even, pltpu.roll(odd, 64, 1)),
                jnp.where(lane < 64, pltpu.roll(even, 64, 1), odd),
            )
            for i in range(2):
                c = 2 * pair + i
                seen = jnp.sum(shade[c, m] * entering[i][None], axis=1)
                image[c, :, lanes] = seen * albedo[HALF * depth + c]
        copy = pltpu.make_async_copy(image.at[:, :, lanes], out.at[:, :, lanes], out_sem.at[m])
        copy.start()
        copies.append(copy)

    wait_blocks(len(NEAR) + 2 * len(FAR), col_send)
    for n, to in enumerate(ends):
        away = hops_between(to, light)

        @pl.when(jnp.logical_and(away > 0, away <= 2))
        def _():
            wait_blocks(1, late_send.at[n])

    @pl.when(late)
    def _():
        wait_blocks(1, relay_sem.at[0])

    @pl.when(jnp.logical_not(late))
    def _():
        wait_blocks(len(NEAR) + 1, relay_sem.at[0])

    @pl.when(has_above)
    def _():
        rim_up.wait_send()

    @pl.when(has_below)
    def _():
        rim_down.wait_send()

    share.wait_send()
    share_lamp.wait_send()

    @pl.when(jnp.logical_or(lamp_up, lamp_down))
    def _():
        pltpu.make_async_copy(lampedge, lampedge, lampedge_sem.at[0]).wait()

    @pl.when(own_part)
    def _():
        part = leaving.at[pl.ds(0, SLABS - 1)]
        pltpu.make_async_copy(part, part, plane_send).wait()

    @pl.when(jnp.logical_not(own_part))
    def _():
        pltpu.make_async_copy(leaving, leaving, plane_send).wait()

    for copy in copies:
        copy.wait()


def local(density, active_list, light_dir, lamp_plane, extinction, blur_weights, albedo):
    f32 = jnp.float32
    anywhere = pl.BlockSpec(memory_space=pl.ANY)
    dma = pltpu.SemaphoreType.DMA
    return pl.pallas_call(
        body,
        out_shape=jax.ShapeDtypeStruct((HALF, SLICES, WIDTH), f32),
        in_specs=[anywhere] * 7,
        out_specs=anywhere,
        scratch_shapes=[
            pltpu.VMEM(active_list.shape, jnp.int32),
            pltpu.SMEM(light_dir.shape, jnp.int32),
            pltpu.SMEM(extinction.shape, f32),
            pltpu.SMEM(blur_weights.shape, f32),
            pltpu.SMEM(albedo.shape, f32),
            pltpu.VMEM((SLICES, ROWS, WIDTH), f32),
            pltpu.VMEM((HALF, ROWS, WIDTH), f32),
            pltpu.VMEM((2, SLICES, ROWS, WIDTH), f32),
            pltpu.VMEM((EIGHTHS, ROWS, 128), f32),
            pltpu.VMEM((2, 8, 128), f32),
            pltpu.VMEM((2, 8, 128), f32),
            pltpu.VMEM((2 * SLABS, ROWS, 128), f32),
            pltpu.VMEM((EIGHTHS, HALF, ROWS, 128), f32),
            pltpu.VMEM((2, HALF, 8, 128), f32),
            pltpu.VMEM((2, 2, ROWS, 128), f32),
            pltpu.VMEM((2, 2, 8, 128), f32),
            pltpu.VMEM((2, SLABS, DEPTH, 128), f32),
            pltpu.VMEM((SLABS, DEPTH, 128), f32),
            pltpu.VMEM((BLOCKS, 4, DEPTH, 128), f32),
            pltpu.VMEM((HALF, BLOCKS, SLICES, DEPTH, 128), f32),
            pltpu.VMEM((2, 25, 8, 128), f32),
            pltpu.VMEM((2, DEPTH + 16, 128), f32),
            pltpu.VMEM((HALF, SLICES, WIDTH), f32),
            dma((10,)), dma(()), dma((4,)), dma(()), dma(()), dma((2,)), dma((2,)), dma((2,)), dma((2,)), dma((2,)), dma((2,)),
            dma(()), dma((BLOCKS,)), dma((BLOCKS,)),
        ],
        compiler_params=pltpu.CompilerParams(
            collective_id=0, has_side_effects=True, vmem_limit_bytes=63 * 1024 * 1024
        ),
        name="march_and_shade",
    )(density, active_list, light_dir, lamp_plane, extinction, blur_weights, albedo)


def solution(mesh):
    in_specs = (
        P("light", "depth", "height"),
        P("depth", None),
        P(),
        P(None, "depth", "height"),
        P(),
        P(),
        P(),
    )
    out_specs = P("depth", "light", "height")
    return jax.shard_map(local, mesh=mesh, in_specs=in_specs, out_specs=out_specs, check_vma=False)
```

```python
import jax
import jax.numpy as jnp
from jax import lax
from jax.experimental import pallas as pl
from jax.experimental.pallas import tpu as pltpu
from jax.sharding import PartitionSpec as P

MESH = pl.DeviceIdType.MESH
LOG2E = 1.4426950408889634
SLICES = 16
SLABS = 16
ROWS = 16
DEPTH = 32
WIDTH = 512
BLOCKS = WIDTH // 128
BRICK_ROWS = 8
EIGHTHS = 8
HALF = 4
BEFORE_RELAY = 0
BEFORE_MARCH = 1
SIDE = 4


def hops(down, right):
    return min(down, SIDE - down) + min(right, SIDE - right)


OTHERS = sorted(
    ((down, right) for down in range(SIDE) for right in range(SIDE) if down or right),
    key=lambda step: -hops(*step),
)
FAR = [step for step in OTHERS if hops(*step) > 2]
NEAR = [step for step in OTHERS if hops(*step) <= 2]


def chip_at(light, step):
    down = lax.rem(lax.div(light, SIDE) + step[0], SIDE)
    return SIDE * down + lax.rem(lax.rem(light, SIDE) + step[1], SIDE)


def half_of(light):
    return 1 - light // EIGHTHS


def eighth_of(light):
    return (light % EIGHTHS // SIDE) * SIDE + (light + 3) % SIDE


def hops_between(one, other):
    total = 0
    for a, b in (
        (one // SIDE, other // SIDE),
        (one % SIDE, other % SIDE),
    ):
        way = lax.rem(a - b + SIDE, SIDE)
        total = total + jnp.minimum(way, SIDE - way)
    return total


def device(light, depth, height):
    return {"light": light, "depth": depth, "height": height}


def windows(block):
    lane = lax.broadcasted_iota(jnp.int32, (block.shape[0], 128), 1)
    parts = [block[:, 128 * m : 128 * m + 128] for m in range(BLOCKS)]
    near = [pltpu.roll(part, 32, 1) for part in parts]
    far = [pltpu.roll(part, 96, 1) for part in parts]
    made = [far[0]]
    for m in range(BLOCKS):
        made.append(near[m] if m == 0 else jnp.where(lane < 32, near[m - 1], near[m]))
        made.append(far[m] if m == BLOCKS - 1 else jnp.where(lane < 96, far[m], far[m + 1]))
    made.append(near[BLOCKS - 1])
    return made


def packed_low(window):
    lane = lax.broadcasted_iota(jnp.int32, (8, 128), 1)
    return jnp.where(lane < 32, window[:8], pltpu.roll(window[8:], 32, 1))


def packed_high(window):
    lane = lax.broadcasted_iota(jnp.int32, (8, 128), 1)
    return jnp.where(lane >= 96, window[:8], pltpu.roll(window[8:], 96, 1))


def spread(rim, turn):
    return jnp.concatenate([rim, pltpu.roll(rim, turn, 1)], axis=0)


def body(
    density, active_hbm, light_dir_hbm, lamp, extinction_hbm, blur_hbm, albedo_hbm,
    out,
    active, light_dir, extinction, blur_weights, albedo, dens, lampv, masked, wins, rims, rims_in, columns, lampwin, lamprim, lampbuf, lampedge, steps, leaving, planes, shade, taps, lifted, image,
    load_sem, col_send, late_send, far_recv, near_recv, relay_sem, up_sem, down_sem, mask_sem, lamp_sem, lampedge_sem, plane_send, plane_recv, out_sem,
):
    light, depth, height = (lax.axis_index(a) for a in ("light", "depth", "height"))
    heights = lax.axis_size("height")
    half, eighth = half_of(light), eighth_of(light)
    sibling = 1 - depth
    has_below, has_above = height > 0, height < heights - 1
    low_edge = jnp.logical_and(eighth == 0, has_below)
    high_edge = jnp.logical_and(eighth == EIGHTHS - 1, has_above)
    mine = 2 * light + depth
    above, below = lax.rem(height + 1, heights), lax.rem(height + heights - 1, heights)
    first = HALF * half + 2 * depth

    chunk = SLICES // 4
    loads = [
        pltpu.make_async_copy(
            density.at[pl.ds(chunk * i, chunk)], dens.at[pl.ds(chunk * i, chunk)], load_sem.at[i]
        )
        for i in range(4)
    ]
    load_active = pltpu.make_async_copy(active_hbm, active, load_sem.at[5])
    load_active.start()
    for load in loads:
        load.start()
    barrier = pltpu.get_barrier_semaphore()

    def greet(to, core, at):
        pl.semaphore_signal(barrier, inc=1, device_id=device(to, core, at), device_id_type=MESH)

    @pl.when(has_below)
    def _():
        greet(light, depth, below)

    @pl.when(has_above)
    def _():
        greet(light, depth, above)

    @pl.when(low_edge)
    def _():
        greet(light, sibling, below)

    @pl.when(high_edge)
    def _():
        greet(light, sibling, above)

    for step in FAR:
        for core in range(2):
            greet(chip_at(light, step), core, height)

    for step in NEAR:
        for core in range(2):
            greet(chip_at(light, step), core, height)
    greet(light, sibling, height)

    load_lamp = pltpu.make_async_copy(lamp.at[pl.ds(HALF * half, HALF)], lampv, load_sem.at[4])
    load_lamp.start()
    load_small = [
        pltpu.make_async_copy(light_dir_hbm, light_dir, load_sem.at[6]),
        pltpu.make_async_copy(extinction_hbm, extinction, load_sem.at[7]),
        pltpu.make_async_copy(blur_hbm, blur_weights, load_sem.at[8]),
        pltpu.make_async_copy(albedo_hbm, albedo, load_sem.at[9]),
    ]
    for load in load_small:
        load.start()

    load_active.wait()
    listed = active[...]
    live = []
    for m in range(BLOCKS):
        brick = light * (BLOCKS * heights) + height * BLOCKS + m
        found = jnp.max(jnp.where(listed == brick, 1.0, 0.0), axis=1, keepdims=True)
        live.append(
            jnp.concatenate(
                [jnp.broadcast_to(found[i : i + 1], (BRICK_ROWS, 128)) for i in range(2)], axis=0
            )
        )
    live = jnp.concatenate(live, axis=1)

    column = jnp.zeros((ROWS, WIDTH), jnp.float32)
    for i in range(4):
        loads[i].wait()
        for x in range(chunk * i, chunk * i + chunk):
            cells = dens[x] * live
            masked[depth, x] = cells
            column = column + cells
    made = windows(column)
    for j in range(EIGHTHS):
        wins[j] = made[j + 1]
    rims[0] = packed_high(made[0])
    rims[1] = packed_low(made[-1])

    lamp_up = jnp.logical_and(eighth == 0, has_above)
    lamp_down = jnp.logical_and(eighth == EIGHTHS - 1, has_below)
    reached = [flag.astype(jnp.int32) for flag in (has_below, has_above, lamp_down, lamp_up)]
    pl.semaphore_wait(barrier, 2 * SLABS - 1 + sum(reached))

    rim_up = pltpu.make_async_remote_copy(
        rims.at[1], rims_in.at[1], up_sem.at[0], up_sem.at[1],
        device_id=device(light, depth, above), device_id_type=MESH,
    )
    rim_down = pltpu.make_async_remote_copy(
        rims.at[0], rims_in.at[0], down_sem.at[0], down_sem.at[1],
        device_id=device(light, depth, below), device_id_type=MESH,
    )

    @pl.when(has_above)
    def _():
        rim_up.start()

    @pl.when(has_below)
    def _():
        rim_down.start()

    def send_window(to, core, arrived, left=col_send):
        pltpu.make_async_remote_copy(
            wins.at[eighth_of(to)], columns.at[mine], left, arrived,
            device_id=device(to, core, height), device_id_type=MESH,
        ).start()

    def at_rim(to):
        return jnp.logical_or(eighth_of(to) == 0, eighth_of(to) == EIGHTHS - 1)

    def send_far(to):
        for core in range(2):
            send_window(to, core, far_recv)

    for step in FAR:
        to = chip_at(light, step)

        @pl.when(jnp.logical_not(at_rim(to)))
        def _():
            send_far(to)

    for step in NEAR:
        to = chip_at(light, step)

        @pl.when(jnp.logical_not(at_rim(to)))
        def _():
            send_window(to, depth, near_recv)

    share = pltpu.make_async_remote_copy(
        masked.at[depth], masked.at[depth], mask_sem.at[0], mask_sem.at[1],
        device_id=device(light, sibling, height), device_id_type=MESH,
    )
    share.start()

    load_lamp.wait()
    for c in range(HALF):
        made = windows(lampv[c])
        for j in range(EIGHTHS):
            lampwin[j, c] = made[j + 1]
        lamprim[0, c] = packed_high(made[0])
        lamprim[1, c] = packed_low(made[-1])
    share_lamp = pltpu.make_async_remote_copy(
        lampwin.at[eighth, pl.ds(2 * sibling, 2)], lampbuf.at[depth], lamp_sem.at[0], lamp_sem.at[1],
        device_id=device(light, sibling, height), device_id_type=MESH,
    )
    share_lamp.start()

    def lamp_over(source, at):
        for to in range(2):
            pltpu.make_async_remote_copy(
                lamprim.at[source, pl.ds(2 * to, 2)], lampedge.at[depth], lampedge_sem.at[0], lampedge_sem.at[1],
                device_id=device(light, to, at), device_id_type=MESH,
            ).start()

    @pl.when(lamp_up)
    def _():
        lamp_over(1, above)

    @pl.when(lamp_down)
    def _():
        lamp_over(0, below)

    lampbuf[depth] = lampwin[eighth, pl.ds(2 * depth, 2)]

    thin = lax.broadcasted_iota(jnp.int32, (ROWS, 128), 1)

    @pl.when(has_below)
    def _():
        rim_up.wait_recv()
        wins[0] = jnp.where(thin < 32, spread(rims_in[1], 96), wins[0])

    @pl.when(has_above)
    def _():
        rim_down.wait_recv()
        wins[EIGHTHS - 1] = jnp.where(thin >= 96, spread(rims_in[0], 32), wins[EIGHTHS - 1])

    ends = [to for to in range(SLABS) if eighth_of(to) in (0, EIGHTHS - 1)]
    for to in ends:

        @pl.when(hops_between(to, light) > 2)
        def _():
            send_far(to)

    for to in ends:
        away = hops_between(to, light)

        @pl.when(jnp.logical_and(away > 0, away <= 2))
        def _():
            send_window(to, depth, near_recv)
            send_window(to, sibling, near_recv, late_send.at[ends.index(to)])

    def relay(block, source):
        pltpu.make_async_remote_copy(
            source, columns.at[block], relay_sem.at[0], relay_sem.at[1],
            device_id=device(light, sibling, height), device_id_type=MESH,
        ).start()

    relay(mine, wins.at[eighth])
    columns[mine] = wins[eighth]

    lane = lax.broadcasted_iota(jnp.int32, (DEPTH, 128), 1)
    row = lax.broadcasted_iota(jnp.int32, (DEPTH, 128), 0)

    share.wait_recv()

    for load in load_small:
        load.wait()
    shown = [HALF * depth + i for i in range(HALF)]
    shown_down = [jnp.full((DEPTH, 128), light_dir[c], jnp.int32) == 1 for c in shown]
    shown_rate = [extinction[c] * -LOG2E for c in shown]

    def shading(m):
        lanes = pl.ds(pl.multiple_of(128 * m, 128), 128)

        def cells_of(x):
            return masked[:, x, :, lanes].reshape(DEPTH, 128)

        total = lax.fori_loop(
            0, SLICES, lambda x, t: t + cells_of(x), jnp.zeros((DEPTH, 128), jnp.float32), unroll=True
        )

        def one(x, running):
            cells = cells_of(x)
            after = running + cells
            behind = total - after
            optical = cells * (6.0 / DEPTH)
            summed = optical
            for step in (1, 2, 4, 8, 16):
                summed = summed + jnp.where(row >= step, pltpu.roll(summed, step, 0), 0.0)
            weight = jnp.exp(optical - summed) * (1.0 - jnp.exp(-optical))
            for i in range(HALF):
                before = jnp.where(shown_down[i], behind, running)
                shade[i, m, x] = jnp.exp2(before * shown_rate[i]) * weight
            return after

        def two(i, running):
            return one(2 * i + 1, one(2 * i, running))

        lax.fori_loop(0, SLICES // 2, two, jnp.zeros((DEPTH, 128), jnp.float32))

    for i in range(2):
        for t in range(25):
            taps[i, t] = jnp.full((8, 128), blur_weights[first + i, t], jnp.float32)

    @pl.loop(0, BEFORE_RELAY)
    def _(m):
        shading(m)

    share_lamp.wait_recv()

    on_edge = jnp.logical_or(low_edge, high_edge)

    @pl.when(on_edge)
    def _():
        pltpu.make_async_copy(lampedge, lampedge, lampedge_sem.at[1]).wait()

    def unpacked(rim):
        return jnp.where(jnp.broadcast_to(eighth == 0, (ROWS, 128)), spread(rim, 96), spread(rim, 32))

    foreign = jnp.logical_or(
        lane < jnp.where(low_edge, 32, 0), lane >= jnp.where(high_edge, 96, 128)
    )
    inside = jnp.logical_and(
        lane >= jnp.where(jnp.logical_and(eighth == 0, height == 0), 32, 0),
        lane < jnp.where(jnp.logical_and(eighth == EIGHTHS - 1, height == heights - 1), 96, 128),
    )
    down = [jnp.full((DEPTH, 128), light_dir[first + i], jnp.int32) == 1 for i in range(2)]
    rate = [extinction[first + i] * -LOG2E for i in range(2)]
    scale = []
    for i in range(2):
        whole = blur_weights[first + i, 0]
        for t in range(1, 25):
            whole = whole + blur_weights[first + i, t]
        scale.append(jnp.where(inside, 1.0 / jnp.full((DEPTH, 128), whole, jnp.float32), 0.0))

    for i in range(2):
        lifted[i] = jnp.zeros((DEPTH + 16, 128), jnp.float32)

    start = []
    for i in range(2):
        own = jnp.concatenate([lampbuf[0, i], lampbuf[1, i]], axis=0)
        other = jnp.concatenate([unpacked(lampedge[0, i]), unpacked(lampedge[1, i])], axis=0)
        start.append(jnp.where(foreign, other, own))
        steps[i, 0] = start[i]
    def wait_blocks(count, semaphore):
        some = columns.at[pl.ds(0, count)]
        pltpu.make_async_copy(some, some, semaphore).wait()

    late = at_rim(light)

    @pl.when(jnp.logical_not(late))
    def _():
        wait_blocks(len(NEAR), near_recv)
        for step in NEAR:
            block = 2 * chip_at(light, step) + depth
            relay(block, columns.at[block])

    @pl.loop(BEFORE_RELAY, BEFORE_MARCH)
    def _(m):
        shading(m)

    @pl.when(late)
    def _():
        wait_blocks(2 * len(NEAR), near_recv)
        wait_blocks(1, relay_sem.at[1])

    @pl.when(jnp.logical_not(late))
    def _():
        wait_blocks(len(NEAR) + 1, relay_sem.at[1])

    wait_blocks(2 * len(FAR), far_recv)
    def column_of(k):
        return columns[pl.ds(2 * k, 2)].reshape(DEPTH, 128)

    def factors(s):
        ahead, back = column_of(s), column_of(SLABS - 1 - s)
        return tuple(
            jnp.exp2(jnp.where(down[i], back, ahead) * rate[i]) * scale[i] for i in range(2)
        )

    def blurred(plane, i):
        lifted[i, 8 : 8 + DEPTH] = plane
        moved = [
            plane if a == 0 else lifted[i, 8 + a : 8 + a + DEPTH] for a in range(-2, 3)
        ]
        moved = [part.reshape(DEPTH // 8, 8, 128) for part in moved]
        total = None
        for b in range(-2, 3):
            term = None
            for a in range(5):
                part = moved[a] * taps[i, 5 * a + b + 2][None]
                term = part if term is None else term + part
            term = term.reshape(DEPTH, 128)
            if b:
                term = pltpu.roll(term, (-b) % 128, 1)
            total = term if total is None else total + term
        return total

    def advance(s, carry):
        plane, factor = carry
        later = factors(s + 1)
        plane = tuple(blurred(plane[i] * factor[i], i) for i in range(2))
        for i in range(2):
            steps[i, s + 1] = plane[i]
        return plane, later

    carry = lax.fori_loop(0, SLABS // 2 - 1, advance, (tuple(start), factors(0)), unroll=True)

    own_part = half == depth
    arrived = plane_recv.at[lax.div(eighth, 2)]
    place = planes.at[lax.div(eighth, 2), 2 * lax.rem(eighth, 2) + depth]

    def send(k):
        @pl.when(jnp.logical_not(jnp.logical_and(k == light, own_part)))
        def _():
            pltpu.make_async_remote_copy(
                leaving.at[k], place, plane_send, arrived,
                device_id=device(k, half, height), device_id_type=MESH,
            ).start()

    def advance_and_send(j, carry):
        s = j + SLABS // 2 - 1
        carry = advance(s, carry)
        late = carry[0]
        early = [steps[i, SLABS - 2 - s] for i in range(2)]
        front = [jnp.where(down[i], early[i], late[i]) for i in range(2)]
        rear = [jnp.where(down[i], late[i], early[i]) for i in range(2)]
        for k, pair in ((SLABS - 2 - s, rear), (s + 1, front)):
            leaving[k] = jnp.where(lane < 64, pltpu.roll(pair[0], 96, 1), pltpu.roll(pair[1], 32, 1))

            @pl.when(hops_between(k, light) > 1)
            def _():
                send(k)

        return carry

    lax.fori_loop(0, SLABS // 2, advance_and_send, carry, unroll=True)

    for step in OTHERS[::-1]:
        if hops(*step) == 1:
            send(chip_at(light, step))

    @pl.when(jnp.logical_not(own_part))
    def _():
        send(light)

    @pl.when(own_part)
    def _():
        pltpu.make_async_copy(leaving.at[light], place, arrived).start()

    @pl.loop(BEFORE_MARCH, BLOCKS)
    def _(m):
        shading(m)


    copies = []
    for m in (1, 2, 3, 0):
        pltpu.make_async_copy(planes.at[m], planes.at[m], plane_recv.at[m]).wait()
        lanes = pl.ds(128 * m, 128)
        for pair in range(2):
            even, odd = planes[m, pair], planes[m, 2 + pair]
            entering = (
                jnp.where(lane < 64, even, pltpu.roll(odd, 64, 1)),
                jnp.where(lane < 64, pltpu.roll(even, 64, 1), odd),
            )
            for i in range(2):
                c = 2 * pair + i
                seen = jnp.sum(shade[c, m] * entering[i][None], axis=1)
                image[c, :, lanes] = seen * albedo[HALF * depth + c]
        copy = pltpu.make_async_copy(image.at[:, :, lanes], out.at[:, :, lanes], out_sem.at[m])
        copy.start()
        copies.append(copy)

    wait_blocks(len(NEAR) + 2 * len(FAR), col_send)
    for n, to in enumerate(ends):
        away = hops_between(to, light)

        @pl.when(jnp.logical_and(away > 0, away <= 2))
        def _():
            wait_blocks(1, late_send.at[n])

    @pl.when(late)
    def _():
        wait_blocks(1, relay_sem.at[0])

    @pl.when(jnp.logical_not(late))
    def _():
        wait_blocks(len(NEAR) + 1, relay_sem.at[0])

    @pl.when(has_above)
    def _():
        rim_up.wait_send()

    @pl.when(has_below)
    def _():
        rim_down.wait_send()

    share.wait_send()
    share_lamp.wait_send()

    @pl.when(jnp.logical_or(lamp_up, lamp_down))
    def _():
        pltpu.make_async_copy(lampedge, lampedge, lampedge_sem.at[0]).wait()

    @pl.when(own_part)
    def _():
        part = leaving.at[pl.ds(0, SLABS - 1)]
        pltpu.make_async_copy(part, part, plane_send).wait()

    @pl.when(jnp.logical_not(own_part))
    def _():
        pltpu.make_async_copy(leaving, leaving, plane_send).wait()

    for copy in copies:
        copy.wait()


def local(density, active_list, light_dir, lamp_plane, extinction, blur_weights, albedo):
    f32 = jnp.float32
    anywhere = pl.BlockSpec(memory_space=pl.ANY)
    dma = pltpu.SemaphoreType.DMA
    return pl.pallas_call(
        body,
        out_shape=jax.ShapeDtypeStruct((HALF, SLICES, WIDTH), f32),
        in_specs=[anywhere] * 7,
        out_specs=anywhere,
        scratch_shapes=[
            pltpu.VMEM(active_list.shape, jnp.int32),
            pltpu.SMEM(light_dir.shape, jnp.int32),
            pltpu.SMEM(extinction.shape, f32),
            pltpu.SMEM(blur_weights.shape, f32),
            pltpu.SMEM(albedo.shape, f32),
            pltpu.VMEM((SLICES, ROWS, WIDTH), f32),
            pltpu.VMEM((HALF, ROWS, WIDTH), f32),
            pltpu.VMEM((2, SLICES, ROWS, WIDTH), f32),
            pltpu.VMEM((EIGHTHS, ROWS, 128), f32),
            pltpu.VMEM((2, 8, 128), f32),
            pltpu.VMEM((2, 8, 128), f32),
            pltpu.VMEM((2 * SLABS, ROWS, 128), f32),
            pltpu.VMEM((EIGHTHS, HALF, ROWS, 128), f32),
            pltpu.VMEM((2, HALF, 8, 128), f32),
            pltpu.VMEM((2, 2, ROWS, 128), f32),
            pltpu.VMEM((2, 2, 8, 128), f32),
            pltpu.VMEM((2, SLABS, DEPTH, 128), f32),
            pltpu.VMEM((SLABS, DEPTH, 128), f32),
            pltpu.VMEM((BLOCKS, 4, DEPTH, 128), f32),
            pltpu.VMEM((HALF, BLOCKS, SLICES, DEPTH, 128), f32),
            pltpu.VMEM((2, 25, 8, 128), f32),
            pltpu.VMEM((2, DEPTH + 16, 128), f32),
            pltpu.VMEM((HALF, SLICES, WIDTH), f32),
            dma((10,)), dma(()), dma((4,)), dma(()), dma(()), dma((2,)), dma((2,)), dma((2,)), dma((2,)), dma((2,)), dma((2,)),
            dma(()), dma((BLOCKS,)), dma((BLOCKS,)),
        ],
        compiler_params=pltpu.CompilerParams(
            collective_id=0, has_side_effects=True, vmem_limit_bytes=63 * 1024 * 1024
        ),
        name="march_and_shade",
    )(density, active_list, light_dir, lamp_plane, extinction, blur_weights, albedo)


def solution(mesh):
    in_specs = (
        P("light", "depth", "height"),
        P("depth", None),
        P(),
        P(None, "depth", "height"),
        P(),
        P(),
        P(),
    )
    out_specs = P("depth", "light", "height")
    return jax.shard_map(local, mesh=mesh, in_specs=in_specs, out_specs=out_specs, check_vma=False)
```

```python
import jax
import jax.numpy as jnp
from jax import lax
from jax.experimental import pallas as pl
from jax.experimental.pallas import tpu as pltpu
from jax.sharding import PartitionSpec as P

MESH = pl.DeviceIdType.MESH
LOG2E = 1.4426950408889634
SLICES = 16
SLABS = 16
ROWS = 16
DEPTH = 32
WIDTH = 512
BLOCKS = WIDTH // 128
BRICK_ROWS = 8
EIGHTHS = 8
HALF = 4
BEFORE_RELAY = 0
BEFORE_MARCH = 1
SIDE = 4


def hops(down, right):
    return min(down, SIDE - down) + min(right, SIDE - right)


OTHERS = sorted(
    ((down, right) for down in range(SIDE) for right in range(SIDE) if down or right),
    key=lambda step: (-hops(*step), -(step[0] == 2) - (step[1] == 2)),
)
FAR = [step for step in OTHERS if hops(*step) > 2]
NEAR = [step for step in OTHERS if hops(*step) <= 2]


def chip_at(light, step):
    down = lax.rem(lax.div(light, SIDE) + step[0], SIDE)
    return SIDE * down + lax.rem(lax.rem(light, SIDE) + step[1], SIDE)


def half_of(light):
    return 1 - light // EIGHTHS


def eighth_of(light):
    return (light % EIGHTHS // SIDE) * SIDE + (light + 3) % SIDE


def hops_between(one, other):
    total = 0
    for a, b in (
        (one // SIDE, other // SIDE),
        (one % SIDE, other % SIDE),
    ):
        way = lax.rem(a - b + SIDE, SIDE)
        total = total + jnp.minimum(way, SIDE - way)
    return total


def device(light, depth, height):
    return {"light": light, "depth": depth, "height": height}


def windows(block):
    lane = lax.broadcasted_iota(jnp.int32, (block.shape[0], 128), 1)
    parts = [block[:, 128 * m : 128 * m + 128] for m in range(BLOCKS)]
    near = [pltpu.roll(part, 32, 1) for part in parts]
    far = [pltpu.roll(part, 96, 1) for part in parts]
    made = [far[0]]
    for m in range(BLOCKS):
        made.append(near[m] if m == 0 else jnp.where(lane < 32, near[m - 1], near[m]))
        made.append(far[m] if m == BLOCKS - 1 else jnp.where(lane < 96, far[m], far[m + 1]))
    made.append(near[BLOCKS - 1])
    return made


def packed_low(window):
    lane = lax.broadcasted_iota(jnp.int32, (8, 128), 1)
    return jnp.where(lane < 32, window[:8], pltpu.roll(window[8:], 32, 1))


def packed_high(window):
    lane = lax.broadcasted_iota(jnp.int32, (8, 128), 1)
    return jnp.where(lane >= 96, window[:8], pltpu.roll(window[8:], 96, 1))


def spread(rim, turn):
    return jnp.concatenate([rim, pltpu.roll(rim, turn, 1)], axis=0)


def body(
    density, active_hbm, light_dir_hbm, lamp, extinction_hbm, blur_hbm, albedo_hbm,
    out,
    active, light_dir, extinction, blur_weights, albedo, dens, lampv, masked, wins, rims, rims_in, columns, lampwin, lamprim, lampbuf, lampedge, steps, leaving, planes, shade, taps, lifted, image,
    load_sem, col_send, late_send, far_recv, near_recv, relay_sem, up_sem, down_sem, mask_sem, lamp_sem, lampedge_sem, plane_send, plane_recv, out_sem,
):
    light, depth, height = (lax.axis_index(a) for a in ("light", "depth", "height"))
    heights = lax.axis_size("height")
    half, eighth = half_of(light), eighth_of(light)
    sibling = 1 - depth
    has_below, has_above = height > 0, height < heights - 1
    low_edge = jnp.logical_and(eighth == 0, has_below)
    high_edge = jnp.logical_and(eighth == EIGHTHS - 1, has_above)
    mine = 2 * light + depth
    above, below = lax.rem(height + 1, heights), lax.rem(height + heights - 1, heights)
    first = HALF * half + 2 * depth

    chunk = SLICES // 4
    loads = [
        pltpu.make_async_copy(
            density.at[pl.ds(chunk * i, chunk)], dens.at[pl.ds(chunk * i, chunk)], load_sem.at[i]
        )
        for i in range(4)
    ]
    load_active = pltpu.make_async_copy(active_hbm, active, load_sem.at[5])
    load_active.start()
    for load in loads:
        load.start()
    barrier = pltpu.get_barrier_semaphore()

    def greet(to, core, at):
        pl.semaphore_signal(barrier, inc=1, device_id=device(to, core, at), device_id_type=MESH)

    @pl.when(has_below)
    def _():
        greet(light, depth, below)

    @pl.when(has_above)
    def _():
        greet(light, depth, above)

    @pl.when(low_edge)
    def _():
        greet(light, sibling, below)

    @pl.when(high_edge)
    def _():
        greet(light, sibling, above)

    for step in FAR:
        for core in range(2):
            greet(chip_at(light, step), core, height)

    for step in NEAR:
        for core in range(2):
            greet(chip_at(light, step), core, height)
    greet(light, sibling, height)

    load_lamp = pltpu.make_async_copy(lamp.at[pl.ds(HALF * half, HALF)], lampv, load_sem.at[4])
    load_lamp.start()
    load_small = [
        pltpu.make_async_copy(light_dir_hbm, light_dir, load_sem.at[6]),
        pltpu.make_async_copy(extinction_hbm, extinction, load_sem.at[7]),
        pltpu.make_async_copy(blur_hbm, blur_weights, load_sem.at[8]),
        pltpu.make_async_copy(albedo_hbm, albedo, load_sem.at[9]),
    ]
    for load in load_small:
        load.start()

    load_active.wait()
    listed = active[...]
    live = []
    for m in range(BLOCKS):
        brick = light * (BLOCKS * heights) + height * BLOCKS + m
        found = jnp.max(jnp.where(listed == brick, 1.0, 0.0), axis=1, keepdims=True)
        live.append(
            jnp.concatenate(
                [jnp.broadcast_to(found[i : i + 1], (BRICK_ROWS, 128)) for i in range(2)], axis=0
            )
        )
    live = jnp.concatenate(live, axis=1)

    column = jnp.zeros((ROWS, WIDTH), jnp.float32)
    for i in range(4):
        loads[i].wait()
        for x in range(chunk * i, chunk * i + chunk):
            cells = dens[x] * live
            masked[depth, x] = cells
            column = column + cells
    made = windows(column)
    for j in range(EIGHTHS):
        wins[j] = made[j + 1]
    rims[0] = packed_high(made[0])
    rims[1] = packed_low(made[-1])

    lamp_up = jnp.logical_and(eighth == 0, has_above)
    lamp_down = jnp.logical_and(eighth == EIGHTHS - 1, has_below)
    reached = [flag.astype(jnp.int32) for flag in (has_below, has_above, lamp_down, lamp_up)]
    pl.semaphore_wait(barrier, 2 * SLABS - 1 + sum(reached))

    rim_up = pltpu.make_async_remote_copy(
        rims.at[1], rims_in.at[1], up_sem.at[0], up_sem.at[1],
        device_id=device(light, depth, above), device_id_type=MESH,
    )
    rim_down = pltpu.make_async_remote_copy(
        rims.at[0], rims_in.at[0], down_sem.at[0], down_sem.at[1],
        device_id=device(light, depth, below), device_id_type=MESH,
    )

    @pl.when(has_above)
    def _():
        rim_up.start()

    @pl.when(has_below)
    def _():
        rim_down.start()

    def send_window(to, core, arrived, left=col_send):
        pltpu.make_async_remote_copy(
            wins.at[eighth_of(to)], columns.at[mine], left, arrived,
            device_id=device(to, core, height), device_id_type=MESH,
        ).start()

    def at_rim(to):
        return jnp.logical_or(eighth_of(to) == 0, eighth_of(to) == EIGHTHS - 1)

    def send_far(to):
        for core in range(2):
            send_window(to, core, far_recv)

    for step in FAR:
        to = chip_at(light, step)

        @pl.when(jnp.logical_not(at_rim(to)))
        def _():
            send_far(to)

    for step in NEAR:
        to = chip_at(light, step)

        @pl.when(jnp.logical_not(at_rim(to)))
        def _():
            send_window(to, depth, near_recv)

    share = pltpu.make_async_remote_copy(
        masked.at[depth], masked.at[depth], mask_sem.at[0], mask_sem.at[1],
        device_id=device(light, sibling, height), device_id_type=MESH,
    )
    share.start()

    load_lamp.wait()
    for c in range(HALF):
        made = windows(lampv[c])
        for j in range(EIGHTHS):
            lampwin[j, c] = made[j + 1]
        lamprim[0, c] = packed_high(made[0])
        lamprim[1, c] = packed_low(made[-1])
    share_lamp = pltpu.make_async_remote_copy(
        lampwin.at[eighth, pl.ds(2 * sibling, 2)], lampbuf.at[depth], lamp_sem.at[0], lamp_sem.at[1],
        device_id=device(light, sibling, height), device_id_type=MESH,
    )
    share_lamp.start()

    def lamp_over(source, at):
        for to in range(2):
            pltpu.make_async_remote_copy(
                lamprim.at[source, pl.ds(2 * to, 2)], lampedge.at[depth], lampedge_sem.at[0], lampedge_sem.at[1],
                device_id=device(light, to, at), device_id_type=MESH,
            ).start()

    @pl.when(lamp_up)
    def _():
        lamp_over(1, above)

    @pl.when(lamp_down)
    def _():
        lamp_over(0, below)

    lampbuf[depth] = lampwin[eighth, pl.ds(2 * depth, 2)]

    thin = lax.broadcasted_iota(jnp.int32, (ROWS, 128), 1)

    @pl.when(has_below)
    def _():
        rim_up.wait_recv()
        wins[0] = jnp.where(thin < 32, spread(rims_in[1], 96), wins[0])

    @pl.when(has_above)
    def _():
        rim_down.wait_recv()
        wins[EIGHTHS - 1] = jnp.where(thin >= 96, spread(rims_in[0], 32), wins[EIGHTHS - 1])

    ends = [to for to in range(SLABS) if eighth_of(to) in (0, EIGHTHS - 1)]
    for to in ends:

        @pl.when(hops_between(to, light) > 2)
        def _():
            send_far(to)

    for to in ends:
        away = hops_between(to, light)

        @pl.when(jnp.logical_and(away > 0, away <= 2))
        def _():
            send_window(to, depth, near_recv)
            send_window(to, sibling, near_recv, late_send.at[ends.index(to)])

    def relay(block, source):
        pltpu.make_async_remote_copy(
            source, columns.at[block], relay_sem.at[0], relay_sem.at[1],
            device_id=device(light, sibling, height), device_id_type=MESH,
        ).start()

    relay(mine, wins.at[eighth])
    columns[mine] = wins[eighth]

    lane = lax.broadcasted_iota(jnp.int32, (DEPTH, 128), 1)
    row = lax.broadcasted_iota(jnp.int32, (DEPTH, 128), 0)

    share.wait_recv()

    for load in load_small:
        load.wait()
    shown = [HALF * depth + i for i in range(HALF)]
    shown_down = [jnp.full((DEPTH, 128), light_dir[c], jnp.int32) == 1 for c in shown]
    shown_rate = [extinction[c] * -LOG2E for c in shown]

    def shading(m):
        lanes = pl.ds(pl.multiple_of(128 * m, 128), 128)

        def cells_of(x):
            return masked[:, x, :, lanes].reshape(DEPTH, 128)

        total = lax.fori_loop(
            0, SLICES, lambda x, t: t + cells_of(x), jnp.zeros((DEPTH, 128), jnp.float32), unroll=True
        )

        def one(x, running):
            cells = cells_of(x)
            after = running + cells
            behind = total - after
            optical = cells * (6.0 / DEPTH)
            summed = optical
            for step in (1, 2, 4, 8, 16):
                summed = summed + jnp.where(row >= step, pltpu.roll(summed, step, 0), 0.0)
            weight = jnp.exp(optical - summed) * (1.0 - jnp.exp(-optical))
            for i in range(HALF):
                before = jnp.where(shown_down[i], behind, running)
                shade[i, m, x] = jnp.exp2(before * shown_rate[i]) * weight
            return after

        def two(i, running):
            return one(2 * i + 1, one(2 * i, running))

        lax.fori_loop(0, SLICES // 2, two, jnp.zeros((DEPTH, 128), jnp.float32))

    for i in range(2):
        for t in range(25):
            taps[i, t] = jnp.full((8, 128), blur_weights[first + i, t], jnp.float32)

    @pl.loop(0, BEFORE_RELAY)
    def _(m):
        shading(m)

    share_lamp.wait_recv()

    on_edge = jnp.logical_or(low_edge, high_edge)

    @pl.when(on_edge)
    def _():
        pltpu.make_async_copy(lampedge, lampedge, lampedge_sem.at[1]).wait()

    def unpacked(rim):
        return jnp.where(jnp.broadcast_to(eighth == 0, (ROWS, 128)), spread(rim, 96), spread(rim, 32))

    foreign = jnp.logical_or(
        lane < jnp.where(low_edge, 32, 0), lane >= jnp.where(high_edge, 96, 128)
    )
    inside = jnp.logical_and(
        lane >= jnp.where(jnp.logical_and(eighth == 0, height == 0), 32, 0),
        lane < jnp.where(jnp.logical_and(eighth == EIGHTHS - 1, height == heights - 1), 96, 128),
    )
    down = [jnp.full((DEPTH, 128), light_dir[first + i], jnp.int32) == 1 for i in range(2)]
    rate = [extinction[first + i] * -LOG2E for i in range(2)]
    scale = []
    for i in range(2):
        whole = blur_weights[first + i, 0]
        for t in range(1, 25):
            whole = whole + blur_weights[first + i, t]
        scale.append(jnp.where(inside, 1.0 / jnp.full((DEPTH, 128), whole, jnp.float32), 0.0))

    for i in range(2):
        lifted[i] = jnp.zeros((DEPTH + 16, 128), jnp.float32)

    start = []
    for i in range(2):
        own = jnp.concatenate([lampbuf[0, i], lampbuf[1, i]], axis=0)
        other = jnp.concatenate([unpacked(lampedge[0, i]), unpacked(lampedge[1, i])], axis=0)
        start.append(jnp.where(foreign, other, own))
        steps[i, 0] = start[i]
    def wait_blocks(count, semaphore):
        some = columns.at[pl.ds(0, count)]
        pltpu.make_async_copy(some, some, semaphore).wait()

    late = at_rim(light)

    @pl.when(jnp.logical_not(late))
    def _():
        wait_blocks(len(NEAR), near_recv)
        for step in NEAR:
            block = 2 * chip_at(light, step) + depth
            relay(block, columns.at[block])

    @pl.loop(BEFORE_RELAY, BEFORE_MARCH)
    def _(m):
        shading(m)

    @pl.when(late)
    def _():
        wait_blocks(2 * len(NEAR), near_recv)
        wait_blocks(1, relay_sem.at[1])

    @pl.when(jnp.logical_not(late))
    def _():
        wait_blocks(len(NEAR) + 1, relay_sem.at[1])

    wait_blocks(2 * len(FAR), far_recv)
    def column_of(k):
        return columns[pl.ds(2 * k, 2)].reshape(DEPTH, 128)

    def factors(s):
        ahead, back = column_of(s), column_of(SLABS - 1 - s)
        return tuple(
            jnp.exp2(jnp.where(down[i], back, ahead) * rate[i]) * scale[i] for i in range(2)
        )

    def blurred(plane, i):
        lifted[i, 8 : 8 + DEPTH] = plane
        moved = [
            plane if a == 0 else lifted[i, 8 + a : 8 + a + DEPTH] for a in range(-2, 3)
        ]
        moved = [part.reshape(DEPTH // 8, 8, 128) for part in moved]
        total = None
        for b in range(-2, 3):
            term = None
            for a in range(5):
                part = moved[a] * taps[i, 5 * a + b + 2][None]
                term = part if term is None else term + part
            term = term.reshape(DEPTH, 128)
            if b:
                term = pltpu.roll(term, (-b) % 128, 1)
            total = term if total is None else total + term
        return total

    def advance(s, carry):
        plane, factor = carry
        later = factors(s + 1)
        plane = tuple(blurred(plane[i] * factor[i], i) for i in range(2))
        for i in range(2):
            steps[i, s + 1] = plane[i]
        return plane, later

    carry = lax.fori_loop(0, SLABS // 2 - 1, advance, (tuple(start), factors(0)), unroll=True)

    own_part = half == depth
    arrived = plane_recv.at[lax.div(eighth, 2)]
    place = planes.at[lax.div(eighth, 2), 2 * lax.rem(eighth, 2) + depth]

    def send(k):
        @pl.when(jnp.logical_not(jnp.logical_and(k == light, own_part)))
        def _():
            pltpu.make_async_remote_copy(
                leaving.at[k], place, plane_send, arrived,
                device_id=device(k, half, height), device_id_type=MESH,
            ).start()

    def advance_and_send(j, carry):
        s = j + SLABS // 2 - 1
        carry = advance(s, carry)
        late = carry[0]
        early = [steps[i, SLABS - 2 - s] for i in range(2)]
        front = [jnp.where(down[i], early[i], late[i]) for i in range(2)]
        rear = [jnp.where(down[i], late[i], early[i]) for i in range(2)]
        for k, pair in ((SLABS - 2 - s, rear), (s + 1, front)):
            leaving[k] = jnp.where(lane < 64, pltpu.roll(pair[0], 96, 1), pltpu.roll(pair[1], 32, 1))

            @pl.when(hops_between(k, light) > 1)
            def _():
                send(k)

        return carry

    lax.fori_loop(0, SLABS // 2, advance_and_send, carry, unroll=True)

    for step in OTHERS[::-1]:
        if hops(*step) == 1:
            send(chip_at(light, step))

    @pl.when(jnp.logical_not(own_part))
    def _():
        send(light)

    @pl.when(own_part)
    def _():
        pltpu.make_async_copy(leaving.at[light], place, arrived).start()

    @pl.loop(BEFORE_MARCH, BLOCKS)
    def _(m):
        shading(m)


    copies = []
    for m in (1, 2, 3, 0):
        pltpu.make_async_copy(planes.at[m], planes.at[m], plane_recv.at[m]).wait()
        lanes = pl.ds(128 * m, 128)
        for pair in range(2):
            even, odd = planes[m, pair], planes[m, 2 + pair]
            entering = (
                jnp.where(lane < 64, even, pltpu.roll(odd, 64, 1)),
                jnp.where(lane < 64, pltpu.roll(even, 64, 1), odd),
            )
            for i in range(2):
                c = 2 * pair + i
                seen = jnp.sum(shade[c, m] * entering[i][None], axis=1)
                image[c, :, lanes] = seen * albedo[HALF * depth + c]
        copy = pltpu.make_async_copy(image.at[:, :, lanes], out.at[:, :, lanes], out_sem.at[m])
        copy.start()
        copies.append(copy)

    wait_blocks(len(NEAR) + 2 * len(FAR), col_send)
    for n, to in enumerate(ends):
        away = hops_between(to, light)

        @pl.when(jnp.logical_and(away > 0, away <= 2))
        def _():
            wait_blocks(1, late_send.at[n])

    @pl.when(late)
    def _():
        wait_blocks(1, relay_sem.at[0])

    @pl.when(jnp.logical_not(late))
    def _():
        wait_blocks(len(NEAR) + 1, relay_sem.at[0])

    @pl.when(has_above)
    def _():
        rim_up.wait_send()

    @pl.when(has_below)
    def _():
        rim_down.wait_send()

    share.wait_send()
    share_lamp.wait_send()

    @pl.when(jnp.logical_or(lamp_up, lamp_down))
    def _():
        pltpu.make_async_copy(lampedge, lampedge, lampedge_sem.at[0]).wait()

    @pl.when(own_part)
    def _():
        part = leaving.at[pl.ds(0, SLABS - 1)]
        pltpu.make_async_copy(part, part, plane_send).wait()

    @pl.when(jnp.logical_not(own_part))
    def _():
        pltpu.make_async_copy(leaving, leaving, plane_send).wait()

    for copy in copies:
        copy.wait()


def local(density, active_list, light_dir, lamp_plane, extinction, blur_weights, albedo):
    f32 = jnp.float32
    anywhere = pl.BlockSpec(memory_space=pl.ANY)
    dma = pltpu.SemaphoreType.DMA
    return pl.pallas_call(
        body,
        out_shape=jax.ShapeDtypeStruct((HALF, SLICES, WIDTH), f32),
        in_specs=[anywhere] * 7,
        out_specs=anywhere,
        scratch_shapes=[
            pltpu.VMEM(active_list.shape, jnp.int32),
            pltpu.SMEM(light_dir.shape, jnp.int32),
            pltpu.SMEM(extinction.shape, f32),
            pltpu.SMEM(blur_weights.shape, f32),
            pltpu.SMEM(albedo.shape, f32),
            pltpu.VMEM((SLICES, ROWS, WIDTH), f32),
            pltpu.VMEM((HALF, ROWS, WIDTH), f32),
            pltpu.VMEM((2, SLICES, ROWS, WIDTH), f32),
            pltpu.VMEM((EIGHTHS, ROWS, 128), f32),
            pltpu.VMEM((2, 8, 128), f32),
            pltpu.VMEM((2, 8, 128), f32),
            pltpu.VMEM((2 * SLABS, ROWS, 128), f32),
            pltpu.VMEM((EIGHTHS, HALF, ROWS, 128), f32),
            pltpu.VMEM((2, HALF, 8, 128), f32),
            pltpu.VMEM((2, 2, ROWS, 128), f32),
            pltpu.VMEM((2, 2, 8, 128), f32),
            pltpu.VMEM((2, SLABS, DEPTH, 128), f32),
            pltpu.VMEM((SLABS, DEPTH, 128), f32),
            pltpu.VMEM((BLOCKS, 4, DEPTH, 128), f32),
            pltpu.VMEM((HALF, BLOCKS, SLICES, DEPTH, 128), f32),
            pltpu.VMEM((2, 25, 8, 128), f32),
            pltpu.VMEM((2, DEPTH + 16, 128), f32),
            pltpu.VMEM((HALF, SLICES, WIDTH), f32),
            dma((10,)), dma(()), dma((4,)), dma(()), dma(()), dma((2,)), dma((2,)), dma((2,)), dma((2,)), dma((2,)), dma((2,)),
            dma(()), dma((BLOCKS,)), dma((BLOCKS,)),
        ],
        compiler_params=pltpu.CompilerParams(
            collective_id=0, has_side_effects=True, vmem_limit_bytes=63 * 1024 * 1024
        ),
        name="march_and_shade",
    )(density, active_list, light_dir, lamp_plane, extinction, blur_weights, albedo)


def solution(mesh):
    in_specs = (
        P("light", "depth", "height"),
        P("depth", None),
        P(),
        P(None, "depth", "height"),
        P(),
        P(),
        P(),
    )
    out_specs = P("depth", "light", "height")
    return jax.shard_map(local, mesh=mesh, in_specs=in_specs, out_specs=out_specs, check_vma=False)
```
